32 devices in a mesh: wide: 8 (over y, x, core), loop: 4 (over z).
Axes of the slice: x: 2, y: 2, z: 4, core: 2. Of those that a mesh axis runs over, the one named last changes fastest.
Arguments:
- feats: bfloat16 [4096, 512], P('loop'), may hold values from -6 to 6
- tiles: bfloat16 [4, 8, 16, 128, 128], P('loop', 'wide'), may hold values from -0.1875 to 0.1875
- tile_rows: int32 [4, 8, 16], P('loop', 'wide'), may hold values from 0 to 7
- tile_cols: int32 [4, 8, 16], P('loop', 'wide'), may hold values from 0 to 3
- tile_count: int32 [4, 8], P('loop', 'wide'), may hold values from 1 to 16, as said below
- w_msg: bfloat16 [512, 512], replicated, may hold values from -0.25 to 0.25
- w_self: bfloat16 [512, 512], replicated, may hold values from -0.25 to 0.25
- readout: float32 [512], replicated, may hold values from -0.6 to 0.6
- labels: int32 [4096], P('loop'), may hold values from 0 to 1
Outputs:
- logits: float32 [4096], P('loop')
- grad_msg: bfloat16 [512, 512], replicated
- grad_self: bfloat16 [512, 512], replicated
The draws below stay inside these ranges and needn't reach their ends.
Inputs may be any that keep to these rules, and one draw needn't show every extreme that they name: `tile_count`: some loop and wide index uses all 16 slots in every draw.
All inputs are finite; a program needn't handle non-finite values.
Results may differ from the reference program's by a relative error of at most 0.02.
Values may be sent and summed in bfloat16 or wider, within the bound.
A program may use at most 64 MiB of HBM per device.

```python
import jax
import jax.numpy as jnp
from jax import lax

D = 512
TB = 128
NODES = 4096
BLOCKS_DEV = 8
COLS_OWN = 1
TILE_DEV = 16
N_WIDE = 8
N_LOOP = 4


def draw_tile_count(key, part):
    low_key, pick_key = jax.random.split(jax.random.fold_in(key, 7))
    counts = jax.random.randint(low_key, (N_LOOP * N_WIDE,), max(1, TILE_DEV // 4), TILE_DEV * 3 // 4 + 1, dtype=jnp.int32)
    busiest = jax.random.randint(pick_key, (), 0, N_LOOP * N_WIDE, dtype=jnp.int32)
    counts = jnp.where(jnp.arange(N_LOOP * N_WIDE, dtype=jnp.int32) == busiest, TILE_DEV, counts)
    return counts.reshape(N_LOOP, N_WIDE).astype(jnp.int32)


def with_ends(result, rng, smallest, top_value):
    longest = result.shape.index(max(result.shape))
    spots = []
    for shift in (0, 1):
        where = [jax.random.randint(jax.random.fold_in(rng, axis), (), 0, length) for axis, length in enumerate(result.shape)]
        where[longest] = (where[longest] + shift) % result.shape[longest]
        spots.append(tuple(where))
    return result.at[spots[0]].set(smallest).at[spots[1]].set(top_value)


def steps_of(key, dims, pieces, low, high):
    loudness = 1.0
    for axis_at, parts in pieces:
        draws = jax.random.uniform(jax.random.fold_in(jax.random.fold_in(key, 6), axis_at), (parts,), jnp.float32, low / len(pieces), high / len(pieces))
        loudness = loudness * jnp.repeat(jnp.exp(draws), dims[axis_at] // parts).reshape((-1,) + (1,) * (len(dims) - 1 - axis_at))
    return loudness


def scatter_about(own_key, shape, width, most, shards=(), held_as=jnp.bfloat16):
    factor_of = steps_of(own_key, shape, shards, -0.22, 0.18) if shards else 1.0
    result = jax.random.normal(own_key, shape, jnp.float32) * width * factor_of
    return jnp.minimum(jnp.maximum(result, -most), most).astype(held_as)


def setup_inputs(seed: int = 0) -> dict:
    streams_of = jax.random.split(jax.random.key(seed), 10)
    feats = scatter_about(streams_of[0], (NODES, D), 1.0, 6.0, ((0, 4),))
    tiles = scatter_about(streams_of[1], (N_LOOP, N_WIDE, TILE_DEV, TB, TB), (8 * TB) ** -0.5, 0.1875, ((0, 4), (1, 8)))
    tile_rows = with_ends(jax.random.randint(streams_of[2], (N_LOOP, N_WIDE, TILE_DEV), 0, BLOCKS_DEV), jax.random.fold_in(streams_of[2], 1), 0, BLOCKS_DEV - 1).astype(jnp.int32)
    tile_cols = with_ends(jax.random.randint(streams_of[3], (N_LOOP, N_WIDE, TILE_DEV), 0, N_LOOP * COLS_OWN), jax.random.fold_in(streams_of[3], 1), 0, (N_LOOP * COLS_OWN) - 1).astype(jnp.int32)
    tile_count = draw_tile_count(jax.random.fold_in(streams_of[9], 71), 0)
    w_msg = scatter_about(streams_of[5], (D, D), D ** -0.5, 0.25)
    w_self = scatter_about(streams_of[6], (D, D), D ** -0.5, 0.25)
    readout = scatter_about(streams_of[7], (D,), 0.1, 0.6, (), jnp.float32)
    labels = with_ends(jax.random.randint(streams_of[8], (NODES,), 0, 2), jax.random.fold_in(streams_of[8], 1), 0, 1).astype(jnp.int32)
    return {"feats": feats, "tiles": tiles, "tile_rows": tile_rows, "tile_cols": tile_cols, "tile_count": tile_count, "w_msg": w_msg, "w_self": w_self, "readout": readout, "labels": labels}


def reference(feats, tiles, tile_rows, tile_cols, tile_count, w_msg, w_self, readout, labels):
    blocks = feats.reshape(N_LOOP, BLOCKS_DEV, TB, D)
    wide_ids = jnp.arange(N_WIDE, dtype=jnp.int32)
    slot_ids = jnp.arange(TILE_DEV, dtype=jnp.int32)
    row_ids = jnp.arange(BLOCKS_DEV, dtype=jnp.int32)

    def one_loop(loop_pos):
        cols_here = tile_cols[loop_pos]
        source = (cols_here // COLS_OWN).astype(jnp.int32)
        sub_block = (cols_here % COLS_OWN).astype(jnp.int32)
        local_block = (wide_ids[:, None] % BLOCKS_DEV + N_WIDE * sub_block).astype(jnp.int32)
        fetched = blocks[source, local_block]
        product = jnp.einsum("wsij,wsjd->wsid", tiles[loop_pos].astype(jnp.float32),
                             fetched.astype(jnp.float32), precision=lax.Precision.HIGHEST)
        valid_slot = slot_ids[None, :] < tile_count[loop_pos][:, None]
        placing = ((tile_rows[loop_pos][:, :, None] == row_ids[None, None, :])
                   & valid_slot[:, :, None]).astype(jnp.float32)
        partial_value = jnp.einsum("wsr,wsid->wrid", placing, product, precision=lax.Precision.HIGHEST)
        partial_value = lax.optimization_barrier(partial_value.astype(jnp.bfloat16))
        return jnp.sum(partial_value.astype(jnp.float32), axis=0).astype(jnp.bfloat16)

    message = lax.map(one_loop, jnp.arange(N_LOOP, dtype=jnp.int32)).reshape(NODES, D)
    pre_act = (jnp.dot(message, w_msg, preferred_element_type=jnp.float32)
               + jnp.dot(feats, w_self, preferred_element_type=jnp.float32))
    hidden = feats.astype(jnp.float32) + jax.nn.silu(pre_act)
    logits = jnp.dot(hidden, readout, precision=lax.Precision.HIGHEST)
    residual_grad = jax.nn.sigmoid(logits) - labels.astype(jnp.float32)
    gate_sig = jax.nn.sigmoid(pre_act)
    pre_grad = (residual_grad[:, None] * readout[None, :] * gate_sig
                * (1.0 + pre_act * (1.0 - gate_sig))).astype(jnp.bfloat16)
    grad_msg = jnp.dot(message.T, pre_grad, preferred_element_type=jnp.float32).astype(jnp.bfloat16)
    grad_self = jnp.dot(feats.T, pre_grad, preferred_element_type=jnp.float32).astype(jnp.bfloat16)
    return (logits, grad_msg, grad_self)
```

```python
import functools

import jax
import jax.numpy as jnp
from jax import lax
from jax.experimental import pallas as pl
from jax.experimental.pallas import tpu as pltpu
from jax.sharding import PartitionSpec as P

CHUNKS = 2
ROW_STEP = 32


def kernel(
    nl, nw, ns, tb,
    feats, tiles, t_rows, t_cols, t_count, w_msg, w_self, readout, labels,
    out_logits, out_grads,
    gath, tiles_v, nf_v, wm_v, ws_v, adj, part, sib_in, plane_out, plane_in, pre, trans,
    g_part, g_sib, g_out, g_in, z_out, z_in, lg_buf,
    local_sem, send_sem, ga_sem, rs_sib_sem, rs_pl_sem, g_sib_sem, g_pl_sem, zr_sem, za_sem,
    ap_sem, as_sem, lg_sem,
):
    f32, bf16 = jnp.float32, jnp.bfloat16
    rows_dev, width = feats.shape
    nb = rows_dev // tb
    nch = nw // 2
    share = rows_dev // nw
    gshare = 2 * width // nw
    cw = width // CHUNKS
    pieces = z_in.shape[2] and gshare // z_in.shape[2]
    prow = z_in.shape[2]
    w = lax.axis_index("wide")
    l = lax.axis_index("loop")
    core = lax.rem(w, 2)
    chip = lax.div(w, 2)
    other = 1 - core
    sib = chip * 2 + other

    def cols(c):
        return pl.ds(c * cw, cw)

    locs = [
        pltpu.make_async_copy(tiles, tiles_v, local_sem.at[0]),
        pltpu.make_async_copy(
            feats.at[pl.ds(pl.multiple_of(w * share, share), share)], nf_v, local_sem.at[1]
        ),
        pltpu.make_async_copy(w_self, ws_v, local_sem.at[2]),
        pltpu.make_async_copy(w_msg, wm_v, local_sem.at[3]),
    ]
    own_rows = pl.ds(pl.multiple_of(lax.rem(w, nb) * tb, tb), tb)
    own_copies = []
    for c in range(CHUNKS):
        own_copies.append(pltpu.make_async_copy(
            feats.at[own_rows, cols(c)],
            gath.at[c, pl.ds(pl.multiple_of(l * tb, tb), tb)],
            local_sem.at[4 + c],
        ))
    for cp in locs + own_copies:
        cp.start()

    barrier = pltpu.get_barrier_semaphore()
    for d in range(1, nw):
        pl.semaphore_signal(barrier, inc=1, device_id={"wide": lax.rem(w + d, nw), "loop": l},
                            device_id_type=pl.DeviceIdType.MESH)
    for d in range(1, nl):
        pl.semaphore_signal(barrier, inc=1, device_id={"wide": w, "loop": lax.rem(l + d, nl)},
                            device_id_type=pl.DeviceIdType.MESH)
    pl.semaphore_wait(barrier, nw + nl - 2)

    sent = []

    def send(src, dst, recv, wide, loop):
        cp = pltpu.make_async_remote_copy(
            src_ref=src, dst_ref=dst, send_sem=send_sem.at[len(sent)], recv_sem=recv,
            device_id={"wide": wide, "loop": loop}, device_id_type=pl.DeviceIdType.MESH,
        )
        cp.start()
        sent.append(cp)
        return cp

    def chip_at(e):
        return lax.rem(chip + e + nch, nch)

    def loop_at(d):
        return lax.rem(l + d + nl, nl)

    ga = []
    for c in range(CHUNKS):
        ga.append([
            send(feats.at[own_rows, cols(c)],
                 gath.at[c, pl.ds(pl.multiple_of(l * tb, tb), tb)],
                 ga_sem.at[c, d - 1], w, loop_at(d))
            for d in range(1, nl)
        ])

    locs[0].wait()
    cell = [
        jnp.where(s < t_count[0], t_rows[s] * nl + t_cols[s], -1) for s in range(ns)
    ]
    group = 4
    steps = tb // ROW_STEP

    def densify(i, carry):
        r = lax.div(i, steps)
        h = lax.rem(i, steps)
        first = r * tb + h * ROW_STEP
        share_id = lax.div(first, share)
        at = lax.div(share_id, 2) * share + lax.rem(first, share)
        for q0 in range(0, nl, group):
            accs = [jnp.zeros((ROW_STEP, tb), f32) for _ in range(group)]
            for s in range(ns):
                t = tiles_v[s, pl.ds(pl.multiple_of(h * ROW_STEP, ROW_STEP), ROW_STEP), :].astype(f32)
                for g in range(group):
                    on = jnp.where(cell[s] == r * nl + q0 + g, 1.0, 0.0).astype(f32)
                    accs[g] = accs[g] + on * t
            for g in range(group):
                adj[lax.rem(share_id, 2), pl.ds(pl.multiple_of(at, ROW_STEP), ROW_STEP),
                    pl.ds((q0 + g) * tb, tb)] = accs[g].astype(bf16)
        return carry

    lax.fori_loop(0, nb * steps, densify, 0)

    locs[1].wait()
    locs[2].wait()
    nf = nf_v[...]
    pre[...] = jnp.dot(nf, ws_v[...], preferred_element_type=f32)

    def put_trans(first, block):
        for k in range(block.shape[0] // gshare):
            j = first // gshare + k
            trans[j % 2, pl.ds((j // 2) * gshare, gshare), :] = block[k * gshare:(k + 1) * gshare]

    put_trans(width, nf.astype(f32).T.astype(bf16))
    label_col = jnp.broadcast_to(
        labels[pl.ds(w, 1), :].astype(f32), (128, share)).T[:, :1]

    sib_cp = []
    for c in range(CHUNKS):
        own_copies[c].wait()
        for cp in ga[c]:
            cp.wait_recv()
        part[c, other] = jnp.dot(adj[other], gath[c], preferred_element_type=f32).astype(bf16)
        sib_cp.append(send(part.at[c, other], sib_in.at[c], rs_sib_sem.at[c], sib, l))
        part[c, core] = jnp.dot(adj[core], gath[c], preferred_element_type=f32).astype(bf16)

    def pair_sum(c, mine, theirs, out):
        out[c] = (mine[c, core].astype(f32) + theirs[c].astype(f32)).astype(bf16)

    def spread(c, out, land, sems, size):
        return [
            send(out.at[c, pl.ds(pl.multiple_of(chip_at(e) * size, size), size)],
                 land.at[c, e - 1], sems.at[c, e - 1], chip_at(e) * 2 + core, l)
            for e in range(1, nch)
        ]

    def total(c, out, land, size):
        acc = out[c, pl.ds(pl.multiple_of(chip * size, size), size), :].astype(f32)
        for e in range(1, nch):
            acc = acc + land[c, e - 1].astype(f32)
        return acc

    pl_cp = []
    for c in range(CHUNKS):
        sib_cp[c].wait_recv()
        pair_sum(c, part, sib_in, plane_out)
        pl_cp.append(spread(c, plane_out, plane_in, rs_pl_sem, share))
    locs[3].wait()
    for c in range(CHUNKS):
        for cp in pl_cp[c]:
            cp.wait_recv()
        msg = total(c, plane_out, plane_in, share).astype(bf16)
        pre[...] += jnp.dot(msg, wm_v[pl.ds(c * cw, cw), :], preferred_element_type=f32)
        put_trans(c * cw, msg.astype(f32).T.astype(bf16))

    act = pre[...]
    gate = jax.nn.sigmoid(act)
    ro = readout[...]
    hidden = nf_v[...].astype(f32) + act * gate
    logit = jnp.sum(hidden * ro, axis=1, keepdims=True)
    resid = jax.nn.sigmoid(logit) - label_col
    pg = (resid * ro * gate * (1.0 + act * (1.0 - gate))).astype(bf16)

    sib_cp = []
    for c in range(CHUNKS):
        pgc = pg[:, c * cw:(c + 1) * cw]
        g_part[c, other] = jnp.dot(trans[other], pgc, preferred_element_type=f32).astype(bf16)
        sib_cp.append(send(g_part.at[c, other], g_sib.at[c], g_sib_sem.at[c], sib, l))
        g_part[c, core] = jnp.dot(trans[core], pgc, preferred_element_type=f32).astype(bf16)

    lg_buf[w] = jnp.broadcast_to(logit, (share, 128)).T[:8, :]

    pl_cp = []
    for c in range(CHUNKS):
        sib_cp[c].wait_recv()
        pair_sum(c, g_part, g_sib, g_out)
        pl_cp.append(spread(c, g_out, g_in, g_pl_sem, gshare))
    lg_cp = [send(lg_buf.at[w], lg_buf.at[w], lg_sem.at[d - 1], lax.rem(w + d, nw), l)
             for d in range(1, nw)]

    zr_cp = []
    for c in range(CHUNKS):
        for cp in pl_cp[c]:
            cp.wait_recv()
        z_out[c] = total(c, g_out, g_in, gshare).astype(bf16)
        cps = []
        for d in range(1, nl):
            src = z_out.at[c]
            if pieces > 1:
                src = z_out.at[c, pl.ds(pl.multiple_of(loop_at(d) * prow, prow), prow)]
            cps.append(send(src, z_in.at[c, l], zr_sem.at[c, d - 1], w, loop_at(d)))
        zr_cp.append(cps)
        if pieces > 1:
            z_in[c, l] = z_out[c, pl.ds(pl.multiple_of(l * prow, prow), prow), :]
        else:
            z_in[c, l] = z_out[c]

    def piece(wide, d):
        at = loop_at(-d) * prow if pieces > 1 else 0
        return wide, pl.ds(pl.multiple_of(at, prow), prow)

    za_cp, ap_cp, as_cp = [], [], []

    def to_plane(c, d):
        who, rws = piece(w, d)
        ref = out_grads.at[who, rws, cols(c)]
        as_cp.append(send(ref, ref, as_sem.at[c, d, 0], sib, l))
        return [send(ref, ref, ap_sem.at[c, d, e - 1], chip_at(e) * 2 + core, l)
                for e in range(1, nch)]

    for c in range(CHUNKS):
        for cp in zr_cp[c]:
            cp.wait_recv()
        acc = z_in[c, 0].astype(f32)
        for k in range(1, nl):
            acc = acc + z_in[c, k].astype(f32)
        who, rws = piece(w, 0)
        out_grads[who, rws, cols(c)] = acc.astype(bf16)
        ref = out_grads.at[who, rws, cols(c)]
        if pieces > 1:
            za_cp.append([send(ref, ref, za_sem.at[c, d - 1], w, loop_at(d))
                          for d in range(1, nl)])
        ap_cp.append([to_plane(c, 0)])
    for d in range(1, pieces):
        for c in range(CHUNKS):
            za_cp[c][d - 1].wait_recv()
            ap_cp[c].append(to_plane(c, d))
    for d in range(pieces):
        for c in range(CHUNKS):
            for e in range(1, nch):
                ap_cp[c][d][e - 1].wait_recv()
                who, rws = piece(chip_at(-e) * 2 + core, d)
                ref = out_grads.at[who, rws, cols(c)]
                as_cp.append(send(ref, ref, as_sem.at[c, d, e], sib, l))

    for cp in lg_cp:
        cp.wait_recv()
    for k in range(nw):
        out_logits[pl.ds(k, 1), :] = lg_buf[k, :1, :]
    for cp in as_cp:
        cp.wait_recv()
    for cp in sent:
        cp.wait_send()


def body(feats, tiles, tile_rows, tile_cols, tile_count, w_msg, w_self, readout, labels):
    rows_dev, width = feats.shape
    tb = tiles.shape[-1]
    ns = tiles.shape[2]
    nw, nl = lax.axis_size("wide"), lax.axis_size("loop")
    nch = nw // 2
    share = rows_dev // nw
    gshare = 2 * width // nw
    cw = width // CHUNKS
    prow = gshare // nl
    if prow < 16:
        prow = gshare
    pieces = gshare // prow
    bf16, f32 = jnp.bfloat16, jnp.float32
    sends = (
        3 * CHUNKS * (nl - 1) + 2 * CHUNKS + 2 * CHUNKS * (nch - 1) + nw - 1
        + CHUNKS * pieces * (nch - 1) + CHUNKS * pieces * nch
    )
    vmem = pl.BlockSpec(memory_space=pltpu.VMEM)
    smem = pl.BlockSpec(memory_space=pltpu.SMEM)
    hbm = pl.BlockSpec(memory_space=pl.ANY)
    dma = pltpu.SemaphoreType.DMA
    logits, grads = pl.pallas_call(
        functools.partial(kernel, nl, nw, ns, tb),
        out_shape=(
            jax.ShapeDtypeStruct((nw, share), f32),
            jax.ShapeDtypeStruct((nw, gshare, width), bf16),
        ),
        in_specs=[hbm, hbm, smem, smem, smem, hbm, hbm, vmem, vmem],
        out_specs=(vmem, vmem),
        scratch_shapes=[
            pltpu.VMEM((CHUNKS, nl * tb, cw), bf16),
            pltpu.VMEM((ns, tb, tb), bf16),
            pltpu.VMEM((share, width), bf16),
            pltpu.VMEM((width, width), bf16),
            pltpu.VMEM((width, width), bf16),
            pltpu.VMEM((2, nch * share, nl * tb), bf16),
            pltpu.VMEM((CHUNKS, 2, nch * share, cw), bf16),
            pltpu.VMEM((CHUNKS, nch * share, cw), bf16),
            pltpu.VMEM((CHUNKS, nch * share, cw), bf16),
            pltpu.VMEM((CHUNKS, nch - 1, share, cw), bf16),
            pltpu.VMEM((share, width), f32),
            pltpu.VMEM((2, nch * gshare, share), bf16),
            pltpu.VMEM((CHUNKS, 2, nch * gshare, cw), bf16),
            pltpu.VMEM((CHUNKS, nch * gshare, cw), bf16),
            pltpu.VMEM((CHUNKS, nch * gshare, cw), bf16),
            pltpu.VMEM((CHUNKS, nch - 1, gshare, cw), bf16),
            pltpu.VMEM((CHUNKS, gshare, cw), bf16),
            pltpu.VMEM((CHUNKS, nl, prow, cw), bf16),
            pltpu.VMEM((nw, 8, share), f32),
            dma((4 + CHUNKS,)),
            dma((sends,)),
            dma((CHUNKS, nl - 1)),
            dma((CHUNKS,)),
            dma((CHUNKS, nch - 1)),
            dma((CHUNKS,)),
            dma((CHUNKS, nch - 1)),
            dma((CHUNKS, nl - 1)),
            dma((CHUNKS, nl - 1)),
            dma((CHUNKS, pieces, nch - 1)),
            dma((CHUNKS, pieces, nch)),
            dma((nw - 1,)),
        ],
        compiler_params=pltpu.CompilerParams(
            collective_id=0, has_side_effects=True, vmem_limit_bytes=40 * 2**20
        ),
    )(
        feats, tiles.reshape(ns, tb, tb), tile_rows.reshape(ns), tile_cols.reshape(ns),
        tile_count.reshape(1), w_msg, w_self, readout.reshape(1, width),
        labels.reshape(nw, share),
    )
    both = grads.reshape(2, width, width)
    return logits.reshape(rows_dev), both[0], both[1]


def solution(mesh):
    placed = (
        P("loop", None),
        P("loop", "wide", None, None, None),
        P("loop", "wide", None),
        P("loop", "wide", None),
        P("loop", "wide"),
        P(),
        P(),
        P(),
        P("loop"),
    )
    return jax.shard_map(
        body, mesh=mesh, in_specs=placed, out_specs=(P("loop"), P(), P()), check_vma=False
    )
```

```python
import functools

import jax
import jax.numpy as jnp
from jax import lax
from jax.experimental import pallas as pl
from jax.experimental.pallas import tpu as pltpu
from jax.sharding import PartitionSpec as P

CHUNKS = 4
G_CHUNKS = 2
ROW_STEP = 32


def kernel(
    nl, nw, ns, tb,
    feats, tiles, rows_in, cols_in, count_in, w_msg, w_self, readout_in, labels_in,
    out_logits, out_grads,
    t_rows, t_cols, t_count, readout, labels,
    gath, tiles_v, nf_v, wm_v, ws_v, adj, part, sib_in, plane_out, plane_in, pre, trans,
    g_part, g_sib, g_out, g_in, z_out, z_in, lg_buf,
    local_sem, send_sem, right_send, left_send, right_sem, left_sem, rs_sib_sem, rs_pl_sem, g_sib_sem, g_pl_sem, zr_sem, za_sem,
    ap_sem, as_sem, lg_sem,
):
    f32, bf16 = jnp.float32, jnp.bfloat16
    rows_dev, width = feats.shape
    nb = rows_dev // tb
    nch = nw // 2
    share = rows_dev // nw
    gshare = 2 * width // nw
    cw = width // CHUNKS
    gw = width // G_CHUNKS
    prow = z_in.shape[2]
    pieces = gshare // prow
    w = lax.axis_index("wide")
    l = lax.axis_index("loop")
    core = lax.rem(w, 2)
    chip = lax.div(w, 2)
    other = 1 - core
    sib = chip * 2 + other

    def cols(c):
        return pl.ds(c * cw, cw)

    def gcols(c):
        return pl.ds(c * gw, gw)

    def block_rows(q):
        return pl.ds(pl.multiple_of(q * tb, tb), tb)

    locs = [
        pltpu.make_async_copy(tiles, tiles_v, local_sem.at[0]),
        pltpu.make_async_copy(
            feats.at[pl.ds(pl.multiple_of(w * share, share), share)], nf_v, local_sem.at[1]
        ),
        pltpu.make_async_copy(w_self, ws_v, local_sem.at[2]),
        pltpu.make_async_copy(w_msg, wm_v, local_sem.at[3]),
        pltpu.make_async_copy(rows_in, t_rows, local_sem.at[4]),
        pltpu.make_async_copy(cols_in, t_cols, local_sem.at[5]),
        pltpu.make_async_copy(readout_in, readout, local_sem.at[6]),
        pltpu.make_async_copy(labels_in, labels, local_sem.at[7]),
        pltpu.make_async_copy(count_in, t_count, local_sem.at[8]),
    ]
    own_rows = pl.ds(pl.multiple_of(lax.rem(w, nb) * tb, tb), tb)
    own_copies = []
    for c in range(CHUNKS):
        own_copies.append(pltpu.make_async_copy(
            feats.at[own_rows, cols(c)],
            gath.at[c, block_rows(l)],
            local_sem.at[9 + c],
        ))
    for cp in locs + own_copies:
        cp.start()

    barrier = pltpu.get_barrier_semaphore()
    for d in range(1, nw):
        pl.semaphore_signal(barrier, inc=1, device_id={"wide": lax.rem(w + d, nw), "loop": l},
                            device_id_type=pl.DeviceIdType.MESH)
    for d in range(1, nl):
        pl.semaphore_signal(barrier, inc=1, device_id={"wide": w, "loop": lax.rem(l + d, nl)},
                            device_id_type=pl.DeviceIdType.MESH)
    pl.semaphore_wait(barrier, nw + nl - 2)

    sent = []

    def send(src, dst, recv, wide, loop):
        cp = pltpu.make_async_remote_copy(
            src_ref=src, dst_ref=dst, send_sem=send_sem.at[len(sent)], recv_sem=recv,
            device_id={"wide": wide, "loop": loop}, device_id_type=pl.DeviceIdType.MESH,
        )
        cp.start()
        sent.append(cp)
        return cp

    def chip_at(e):
        return lax.rem(chip + e + nch, nch)

    def loop_at(d):
        return lax.rem(l + d + nl, nl)

    maybe_sent = []

    def send_if(on, src, c, block, dist, to_right, step):
        send_s = (right_send if to_right else left_send).at[c, dist - 1]
        recv_s = (right_sem if to_right else left_sem).at[c, dist - 1]

        def make():
            return pltpu.make_async_remote_copy(
                src_ref=src(), dst_ref=gath.at[c, block_rows(block)], send_sem=send_s, recv_sem=recv_s,
                device_id={"wide": w, "loop": l + step if to_right else l - step},
                device_id_type=pl.DeviceIdType.MESH,
            )

        @pl.when(on)
        def _():
            make().start()

        maybe_sent.append((on, make))

    def wait_if(on, c, dist, from_left):
        @pl.when(on)
        def _():
            ref = gath.at[c, block_rows(l - dist if from_left else l + dist)]
            pltpu.make_async_remote_copy(
                src_ref=ref, dst_ref=ref, send_sem=send_sem.at[0],
                recv_sem=(right_sem if from_left else left_sem).at[c, dist - 1],
                device_id={"wide": w, "loop": l - 1 if from_left else l + 1},
                device_id_type=pl.DeviceIdType.MESH,
            ).wait_recv()

    relayed = range(2, nl - 1)
    for c in range(CHUNKS):
        for d in (2, 1):
            if d < nl:
                own = functools.partial(lambda c: feats.at[own_rows, cols(c)], c)
                send_if(l + d < nl, own, c, l, d, True, d)
                send_if(l >= d, own, c, l, d, False, d)

    def relay(c):
        for t in relayed:
            wait_if(l >= t, c, t, True)
            send_if(jnp.logical_and(l >= t, l + 1 < nl),
                    functools.partial(lambda c, t: gath.at[c, block_rows(l - t)], c, t),
                    c, l - t, t + 1, True, 1)
            wait_if(l + t < nl, c, t, False)
            send_if(jnp.logical_and(l + t < nl, l >= 1),
                    functools.partial(lambda c, t: gath.at[c, block_rows(l + t)], c, t),
                    c, l + t, t + 1, False, 1)

    def gathered(c):
        own_copies[c].wait()
        for t in range(1, nl):
            if t not in relayed:
                wait_if(l >= t, c, t, True)
                wait_if(l + t < nl, c, t, False)

    for k in (0, 4, 5, 8):
        locs[k].wait()
    cell = [
        jnp.where(s < t_count[0], t_rows[s] * nl + t_cols[s], -1) for s in range(ns)
    ]
    group = 4
    steps = tb // ROW_STEP

    def densify(i, carry):
        r = lax.div(i, steps)
        h = lax.rem(i, steps)
        first = r * tb + h * ROW_STEP
        share_id = lax.div(first, share)
        at = lax.div(share_id, 2) * share + lax.rem(first, share)
        for q0 in range(0, nl, group):
            accs = [jnp.zeros((ROW_STEP, tb), f32) for _ in range(group)]
            for s in range(ns):
                t = tiles_v[s, pl.ds(pl.multiple_of(h * ROW_STEP, ROW_STEP), ROW_STEP), :].astype(f32)
                for g in range(group):
                    on = jnp.where(cell[s] == r * nl + q0 + g, 1.0, 0.0).astype(f32)
                    accs[g] = accs[g] + on * t
            for g in range(group):
                adj[lax.rem(share_id, 2), pl.ds(pl.multiple_of(at, ROW_STEP), ROW_STEP),
                    pl.ds((q0 + g) * tb, tb)] = accs[g].astype(bf16)
        return carry

    lax.fori_loop(0, nb * steps // 2, densify, 0)
    relay(0)
    lax.fori_loop(nb * steps // 2, nb * steps, densify, 0)
    relay(1)

    sib_cp, pl_cp = [], []

    def partial_of(c):
        gathered(c)
        part[c, other] = jnp.dot(adj[other], gath[c], preferred_element_type=f32).astype(bf16)
        sib_cp.append(send(part.at[c, other], sib_in.at[c], rs_sib_sem.at[c], sib, l))
        part[c, core] = jnp.dot(adj[core], gath[c], preferred_element_type=f32).astype(bf16)

    def pair_sum(c, mine, theirs, out):
        out[c] = (mine[c, core].astype(f32) + theirs[c].astype(f32)).astype(bf16)

    def spread(c, out, land, sems, size):
        return [
            send(out.at[c, pl.ds(pl.multiple_of(chip_at(e) * size, size), size)],
                 land.at[c, e - 1], sems.at[c, e - 1], chip_at(e) * 2 + core, l)
            for e in range(1, nch)
        ]

    def total(c, out, land, size):
        acc = out[c, pl.ds(pl.multiple_of(chip * size, size), size), :].astype(f32)
        for e in range(1, nch):
            acc = acc + land[c, e - 1].astype(f32)
        return acc

    def to_chips(c):
        sib_cp[c].wait_recv()
        pair_sum(c, part, sib_in, plane_out)
        pl_cp.append(spread(c, plane_out, plane_in, rs_pl_sem, share))

    def put_trans(first, block):
        for k in range(block.shape[0] // gshare):
            j = first // gshare + k
            trans[j % 2, pl.ds((j // 2) * gshare, gshare), :] = block[k * gshare:(k + 1) * gshare]

    partial_of(0)
    for c in range(2, CHUNKS):
        relay(c)
        partial_of(c - 1)
        to_chips(c - 2)
    partial_of(CHUNKS - 1)
    to_chips(CHUNKS - 2)
    to_chips(CHUNKS - 1)

    for k in (1, 2, 3, 6, 7):
        locs[k].wait()
    nf = nf_v[...]
    pre[...] = jnp.dot(nf, ws_v[...], preferred_element_type=f32)
    put_trans(width, nf.astype(f32).T.astype(bf16))
    label_col = jnp.broadcast_to(
        labels[pl.ds(w, 1), :].astype(f32), (128, share)).T[:, :1]

    for c in range(CHUNKS):
        for cp in pl_cp[c]:
            cp.wait_recv()
        msg = total(c, plane_out, plane_in, share).astype(bf16)
        pre[...] += jnp.dot(msg, wm_v[pl.ds(c * cw, cw), :], preferred_element_type=f32)
        put_trans(c * cw, msg.astype(f32).T.astype(bf16))

    act = pre[...]
    gate = jax.nn.sigmoid(act)
    ro = readout[...]
    hidden = nf_v[...].astype(f32) + act * gate
    logit = jnp.sum(hidden * ro, axis=1, keepdims=True)
    resid = jax.nn.sigmoid(logit) - label_col
    pg = (resid * ro * gate * (1.0 + act * (1.0 - gate))).astype(bf16)

    sib_cp = []
    for c in range(G_CHUNKS):
        pgc = pg[:, c * gw:(c + 1) * gw]
        g_part[c, other] = jnp.dot(trans[other], pgc, preferred_element_type=f32).astype(bf16)
        sib_cp.append(send(g_part.at[c, other], g_sib.at[c], g_sib_sem.at[c], sib, l))
        g_part[c, core] = jnp.dot(trans[core], pgc, preferred_element_type=f32).astype(bf16)

    lg_buf[w] = jnp.broadcast_to(logit, (share, 128)).T[:8, :]

    pl_cp = []
    for c in range(G_CHUNKS):
        sib_cp[c].wait_recv()
        pair_sum(c, g_part, g_sib, g_out)
        pl_cp.append(spread(c, g_out, g_in, g_pl_sem, gshare))
    lg_cp = [send(lg_buf.at[w], lg_buf.at[w], lg_sem.at[d - 1], lax.rem(w + d, nw), l)
             for d in range(1, nw)]

    zr_cp = []
    for c in range(G_CHUNKS):
        for cp in pl_cp[c]:
            cp.wait_recv()
        z_out[c] = total(c, g_out, g_in, gshare).astype(bf16)
        cps = []
        for d in range(1, nl):
            src = z_out.at[c]
            if pieces > 1:
                src = z_out.at[c, pl.ds(pl.multiple_of(loop_at(d) * prow, prow), prow)]
            cps.append(send(src, z_in.at[c, l], zr_sem.at[c, d - 1], w, loop_at(d)))
        zr_cp.append(cps)
        if pieces > 1:
            z_in[c, l] = z_out[c, pl.ds(pl.multiple_of(l * prow, prow), prow), :]
        else:
            z_in[c, l] = z_out[c]

    def piece(wide, d):
        at = loop_at(-d) * prow if pieces > 1 else 0
        return wide, pl.ds(pl.multiple_of(at, prow), prow)

    za_cp, ap_cp, as_cp = [], [], []

    def to_plane(c, d):
        who, rws = piece(w, d)
        ref = out_grads.at[who, rws, gcols(c)]
        as_cp.append(send(ref, ref, as_sem.at[c, d, 0], sib, l))
        return [send(ref, ref, ap_sem.at[c, d, e - 1], chip_at(e) * 2 + core, l)
                for e in range(1, nch)]

    for c in range(G_CHUNKS):
        for cp in zr_cp[c]:
            cp.wait_recv()
        acc = z_in[c, 0].astype(f32)
        for k in range(1, nl):
            acc = acc + z_in[c, k].astype(f32)
        who, rws = piece(w, 0)
        out_grads[who, rws, gcols(c)] = acc.astype(bf16)
        ref = out_grads.at[who, rws, gcols(c)]
        if pieces > 1:
            za_cp.append([send(ref, ref, za_sem.at[c, d - 1], w, loop_at(d))
                          for d in range(1, nl)])
        ap_cp.append([to_plane(c, 0)])
    for d in range(1, pieces):
        for c in range(G_CHUNKS):
            za_cp[c][d - 1].wait_recv()
            ap_cp[c].append(to_plane(c, d))
    for d in range(pieces):
        for c in range(G_CHUNKS):
            for e in range(1, nch):
                ap_cp[c][d][e - 1].wait_recv()
                who, rws = piece(chip_at(-e) * 2 + core, d)
                ref = out_grads.at[who, rws, gcols(c)]
                as_cp.append(send(ref, ref, as_sem.at[c, d, e], sib, l))

    for cp in lg_cp:
        cp.wait_recv()
    for k in range(nw):
        out_logits[pl.ds(k, 1), :] = lg_buf[k, :1, :]
    for cp in as_cp:
        cp.wait_recv()
    for cp in sent:
        cp.wait_send()
    for on, make in maybe_sent:
        pl.when(on)(functools.partial(lambda make: make().wait_send(), make))


def body(feats, tiles, tile_rows, tile_cols, tile_count, w_msg, w_self, readout, labels):
    rows_dev, width = feats.shape
    tb = tiles.shape[-1]
    ns = tiles.shape[2]
    nw, nl = lax.axis_size("wide"), lax.axis_size("loop")
    nch = nw // 2
    share = rows_dev // nw
    gshare = 2 * width // nw
    cw = width // CHUNKS
    gw = width // G_CHUNKS
    prow = gshare // nl
    if prow < 16:
        prow = gshare
    pieces = gshare // prow
    bf16, f32 = jnp.bfloat16, jnp.float32
    sends = (
        CHUNKS * nch + G_CHUNKS * nch + nw - 1 + 2 * G_CHUNKS * (nl - 1)
        + G_CHUNKS * pieces * (2 * nch - 1)
    )
    vmem = pl.BlockSpec(memory_space=pltpu.VMEM)
    hbm = pl.BlockSpec(memory_space=pltpu.HBM)
    dma = pltpu.SemaphoreType.DMA
    logits, grads = pl.pallas_call(
        functools.partial(kernel, nl, nw, ns, tb),
        out_shape=(
            jax.ShapeDtypeStruct((nw, share), f32),
            jax.ShapeDtypeStruct((nw, gshare, width), bf16),
        ),
        in_specs=[hbm] * 9,
        out_specs=(vmem, vmem),
        scratch_shapes=[
            pltpu.SMEM((ns,), jnp.int32),
            pltpu.SMEM((ns,), jnp.int32),
            pltpu.SMEM((1,), jnp.int32),
            pltpu.VMEM((1, width), f32),
            pltpu.VMEM((nw, share), jnp.int32),
            pltpu.VMEM((CHUNKS, nl * tb, cw), bf16),
            pltpu.VMEM((ns, tb, tb), bf16),
            pltpu.VMEM((share, width), bf16),
            pltpu.VMEM((width, width), bf16),
            pltpu.VMEM((width, width), bf16),
            pltpu.VMEM((2, nch * share, nl * tb), bf16),
            pltpu.VMEM((CHUNKS, 2, nch * share, cw), bf16),
            pltpu.VMEM((CHUNKS, nch * share, cw), bf16),
            pltpu.VMEM((CHUNKS, nch * share, cw), bf16),
            pltpu.VMEM((CHUNKS, nch - 1, share, cw), bf16),
            pltpu.VMEM((share, width), f32),
            pltpu.VMEM((2, nch * gshare, share), bf16),
            pltpu.VMEM((G_CHUNKS, 2, nch * gshare, gw), bf16),
            pltpu.VMEM((G_CHUNKS, nch * gshare, gw), bf16),
            pltpu.VMEM((G_CHUNKS, nch * gshare, gw), bf16),
            pltpu.VMEM((G_CHUNKS, nch - 1, gshare, gw), bf16),
            pltpu.VMEM((G_CHUNKS, gshare, gw), bf16),
            pltpu.VMEM((G_CHUNKS, nl, prow, gw), bf16),
            pltpu.VMEM((nw, 8, share), f32),
            dma((9 + CHUNKS,)),
            dma((sends,)),
            dma((CHUNKS, nl - 1)),
            dma((CHUNKS, nl - 1)),
            dma((CHUNKS, nl - 1)),
            dma((CHUNKS, nl - 1)),
            dma((CHUNKS,)),
            dma((CHUNKS, nch - 1)),
            dma((G_CHUNKS,)),
            dma((G_CHUNKS, nch - 1)),
            dma((G_CHUNKS, nl - 1)),
            dma((G_CHUNKS, nl - 1)),
            dma((G_CHUNKS, pieces, nch - 1)),
            dma((G_CHUNKS, pieces, nch)),
            dma((nw - 1,)),
        ],
        compiler_params=pltpu.CompilerParams(
            collective_id=0, has_side_effects=True, vmem_limit_bytes=40 * 2**20
        ),
    )(
        feats, tiles.reshape(ns, tb, tb), tile_rows.reshape(ns), tile_cols.reshape(ns),
        tile_count.reshape(1), w_msg, w_self, readout.reshape(1, width),
        labels.reshape(nw, share),
    )
    both = grads.reshape(2, width, width)
    return logits.reshape(rows_dev), both[0], both[1]


def solution(mesh):
    placed = (
        P("loop", None),
        P("loop", "wide", None, None, None),
        P("loop", "wide", None),
        P("loop", "wide", None),
        P("loop", "wide"),
        P(),
        P(),
        P(),
        P("loop"),
    )
    return jax.shard_map(
        body, mesh=mesh, in_specs=placed, out_specs=(P("loop"), P(), P()), check_vma=False
    )
```

```python
import functools

import jax
import jax.numpy as jnp
from jax import lax
from jax.experimental import pallas as pl
from jax.experimental.pallas import tpu as pltpu
from jax.sharding import PartitionSpec as P

CHUNKS = 4
G_CHUNKS = 2
ROW_STEP = 32


def kernel(
    nl, nw, ns, tb,
    feats, tiles, rows_in, cols_in, count_in, w_msg, w_self, readout_in, labels_in,
    out_logits, out_grads,
    t_rows, t_cols, t_count, readout, labels,
    gath, tiles_v, nf2, msg2, pg2, wm_v, ws_v, adj, part, sib_in, plane_out, plane_in, pre, trans,
    g_out, g_in, z_out, z_in, lg_buf,
    local_sem, send_sem, right_send, left_send, right_sem, left_sem, rs_sib_sem, rs_pl_sem, msg_sem, pg_sem, g_pl_sem, zr_sem, za_sem,
    ap_sem, as_sem, lg_sem,
):
    f32, bf16 = jnp.float32, jnp.bfloat16
    rows_dev, width = feats.shape
    nb = rows_dev // tb
    nch = nw // 2
    share = rows_dev // nw
    gshare = width // nch
    cw = width // CHUNKS
    gw = width // G_CHUNKS
    prow = z_in.shape[2]
    pieces = gshare // prow
    w = lax.axis_index("wide")
    l = lax.axis_index("loop")
    core = lax.rem(w, 2)
    chip = lax.div(w, 2)
    other = 1 - core
    sib = chip * 2 + other

    def cols(c):
        return pl.ds(c * cw, cw)

    def gcols(c):
        return pl.ds(c * gw, gw)

    def block_rows(q):
        return pl.ds(pl.multiple_of(q * tb, tb), tb)

    locs = [
        pltpu.make_async_copy(tiles, tiles_v, local_sem.at[0]),
        pltpu.make_async_copy(
            feats.at[pl.ds(pl.multiple_of(chip * 2 * share, 2 * share), 2 * share)], nf2,
            local_sem.at[1],
        ),
        pltpu.make_async_copy(w_self, ws_v, local_sem.at[2]),
        pltpu.make_async_copy(w_msg, wm_v, local_sem.at[3]),
        pltpu.make_async_copy(rows_in, t_rows, local_sem.at[4]),
        pltpu.make_async_copy(cols_in, t_cols, local_sem.at[5]),
        pltpu.make_async_copy(readout_in, readout, local_sem.at[6]),
        pltpu.make_async_copy(labels_in, labels, local_sem.at[7]),
        pltpu.make_async_copy(count_in, t_count, local_sem.at[8]),
    ]
    own_rows = pl.ds(pl.multiple_of(lax.rem(w, nb) * tb, tb), tb)
    own_copies = []
    for c in range(CHUNKS):
        own_copies.append(pltpu.make_async_copy(
            feats.at[own_rows, cols(c)],
            gath.at[c, block_rows(l)],
            local_sem.at[9 + c],
        ))
    for cp in locs + own_copies:
        cp.start()

    barrier = pltpu.get_barrier_semaphore()
    for d in range(1, nw):
        pl.semaphore_signal(barrier, inc=1, device_id={"wide": lax.rem(w + d, nw), "loop": l},
                            device_id_type=pl.DeviceIdType.MESH)
    for d in range(1, nl):
        pl.semaphore_signal(barrier, inc=1, device_id={"wide": w, "loop": lax.rem(l + d, nl)},
                            device_id_type=pl.DeviceIdType.MESH)
    pl.semaphore_wait(barrier, nw + nl - 2)

    sent = []

    def send(src, dst, recv, wide, loop):
        cp = pltpu.make_async_remote_copy(
            src_ref=src, dst_ref=dst, send_sem=send_sem.at[len(sent)], recv_sem=recv,
            device_id={"wide": wide, "loop": loop}, device_id_type=pl.DeviceIdType.MESH,
        )
        cp.start()
        sent.append(cp)
        return cp

    def chip_at(e):
        return lax.rem(chip + e + nch, nch)

    def loop_at(d):
        return lax.rem(l + d + nl, nl)

    maybe_sent = []

    def send_if(on, src, c, block, dist, to_right, step):
        send_s = (right_send if to_right else left_send).at[c, dist - 1]
        recv_s = (right_sem if to_right else left_sem).at[c, dist - 1]

        def make():
            return pltpu.make_async_remote_copy(
                src_ref=src(), dst_ref=gath.at[c, block_rows(block)], send_sem=send_s, recv_sem=recv_s,
                device_id={"wide": w, "loop": l + step if to_right else l - step},
                device_id_type=pl.DeviceIdType.MESH,
            )

        @pl.when(on)
        def _():
            make().start()

        maybe_sent.append((on, make))

    def wait_if(on, c, dist, from_left):
        @pl.when(on)
        def _():
            ref = gath.at[c, block_rows(l - dist if from_left else l + dist)]
            pltpu.make_async_remote_copy(
                src_ref=ref, dst_ref=ref, send_sem=send_sem.at[0],
                recv_sem=(right_sem if from_left else left_sem).at[c, dist - 1],
                device_id={"wide": w, "loop": l - 1 if from_left else l + 1},
                device_id_type=pl.DeviceIdType.MESH,
            ).wait_recv()

    relayed = range(2, nl - 1)
    for c in range(CHUNKS):
        for d in (2, 1):
            if d < nl:
                own = functools.partial(lambda c: feats.at[own_rows, cols(c)], c)
                send_if(l + d < nl, own, c, l, d, True, d)
                send_if(l >= d, own, c, l, d, False, d)

    def relay(c):
        for t in relayed:
            wait_if(l >= t, c, t, True)
            send_if(jnp.logical_and(l >= t, l + 1 < nl),
                    functools.partial(lambda c, t: gath.at[c, block_rows(l - t)], c, t),
                    c, l - t, t + 1, True, 1)
            wait_if(l + t < nl, c, t, False)
            send_if(jnp.logical_and(l + t < nl, l >= 1),
                    functools.partial(lambda c, t: gath.at[c, block_rows(l + t)], c, t),
                    c, l + t, t + 1, False, 1)

    def gathered(c):
        own_copies[c].wait()
        for t in range(1, nl):
            if t not in relayed:
                wait_if(l >= t, c, t, True)
                wait_if(l + t < nl, c, t, False)

    for k in (0, 4, 5, 8):
        locs[k].wait()
    cell = [
        jnp.where(s < t_count[0], t_rows[s] * nl + t_cols[s], -1) for s in range(ns)
    ]
    group = 4
    steps = tb // ROW_STEP

    def densify(i, carry):
        r = lax.div(i, steps)
        h = lax.rem(i, steps)
        first = r * tb + h * ROW_STEP
        share_id = lax.div(first, share)
        at = lax.div(share_id, 2) * share + lax.rem(first, share)
        for q0 in range(0, nl, group):
            accs = [jnp.zeros((ROW_STEP, tb), f32) for _ in range(group)]
            for s in range(ns):
                t = tiles_v[s, pl.ds(pl.multiple_of(h * ROW_STEP, ROW_STEP), ROW_STEP), :].astype(f32)
                for g in range(group):
                    on = jnp.where(cell[s] == r * nl + q0 + g, 1.0, 0.0).astype(f32)
                    accs[g] = accs[g] + on * t
            for g in range(group):
                adj[lax.rem(share_id, 2), pl.ds(pl.multiple_of(at, ROW_STEP), ROW_STEP),
                    pl.ds((q0 + g) * tb, tb)] = accs[g].astype(bf16)
        return carry

    lax.fori_loop(0, nb * steps // 2, densify, 0)
    relay(0)
    lax.fori_loop(nb * steps // 2, nb * steps, densify, 0)
    relay(1)

    sib_cp, pl_cp = [], []

    def partial_of(c):
        gathered(c)
        part[c, other] = jnp.dot(adj[other], gath[c], preferred_element_type=f32).astype(bf16)
        sib_cp.append(send(part.at[c, other], sib_in.at[c], rs_sib_sem.at[c], sib, l))
        part[c, core] = jnp.dot(adj[core], gath[c], preferred_element_type=f32).astype(bf16)

    def pair_sum(c, mine, theirs, out):
        out[c] = (mine[c, core].astype(f32) + theirs[c].astype(f32)).astype(bf16)

    def spread(c, out, land, sems, size):
        return [
            send(out.at[c, pl.ds(pl.multiple_of(chip_at(e) * size, size), size)],
                 land.at[c, e - 1], sems.at[c, e - 1], chip_at(e) * 2 + core, l)
            for e in range(1, nch)
        ]

    def total(c, out, land, size):
        acc = out[c, pl.ds(pl.multiple_of(chip * size, size), size), :].astype(f32)
        for e in range(1, nch):
            acc = acc + land[c, e - 1].astype(f32)
        return acc

    def to_chips(c):
        sib_cp[c].wait_recv()
        pair_sum(c, part, sib_in, plane_out)
        pl_cp.append(spread(c, plane_out, plane_in, rs_pl_sem, share))

    partial_of(0)
    for c in range(2, CHUNKS):
        relay(c)
        partial_of(c - 1)
        to_chips(c - 2)
    partial_of(CHUNKS - 1)
    to_chips(CHUNKS - 2)
    to_chips(CHUNKS - 1)

    for k in (1, 2, 3, 6, 7):
        locs[k].wait()
    mine = pl.ds(pl.multiple_of(core * share, share), share)
    nf = nf2[mine, :]
    pre[...] = jnp.dot(nf, ws_v[...], preferred_element_type=f32)

    @pl.when(core == 1)
    def _():
        trans[...] = nf2[...].astype(f32).T.astype(bf16)

    label_col = jnp.broadcast_to(
        labels[pl.ds(w, 1), :].astype(f32), (128, share)).T[:, :1]

    msg_cp = []
    for c in range(CHUNKS):
        for cp in pl_cp[c]:
            cp.wait_recv()
        msg = total(c, plane_out, plane_in, share).astype(bf16)
        pre[...] += jnp.dot(msg, wm_v[pl.ds(c * cw, cw), :], preferred_element_type=f32)
        msg2[mine, cols(c)] = msg
        ref = msg2.at[mine, cols(c)]
        msg_cp.append(send(ref, ref, msg_sem.at[c], sib, l))

    act = pre[...]
    gate = jax.nn.sigmoid(act)
    ro = readout[...]
    hidden = nf.astype(f32) + act * gate
    logit = jnp.sum(hidden * ro, axis=1, keepdims=True)
    resid = jax.nn.sigmoid(logit) - label_col
    pg = (resid * ro * gate * (1.0 + act * (1.0 - gate))).astype(bf16)

    pg_cp = []
    for c in range(G_CHUNKS):
        pg2[c, mine, :] = pg[:, c * gw:(c + 1) * gw]
        ref = pg2.at[c, mine]
        pg_cp.append(send(ref, ref, pg_sem.at[c], sib, l))
    for cp in msg_cp:
        cp.wait_recv()

    @pl.when(core == 0)
    def _():
        trans[...] = msg2[...].astype(f32).T.astype(bf16)

    pl_cp = []
    for c in range(G_CHUNKS):
        pg_cp[c].wait_recv()
        g_out[c] = jnp.dot(trans[...], pg2[c], preferred_element_type=f32).astype(bf16)
        pl_cp.append(spread(c, g_out, g_in, g_pl_sem, gshare))
    lg_buf[w] = jnp.broadcast_to(logit, (share, 128)).T[:8, :]
    lg_cp = [send(lg_buf.at[w], lg_buf.at[w], lg_sem.at[d - 1], lax.rem(w + d, nw), l)
             for d in range(1, nw)]

    zr_cp = []
    for c in range(G_CHUNKS):
        for cp in pl_cp[c]:
            cp.wait_recv()
        z_out[c] = total(c, g_out, g_in, gshare).astype(bf16)
        cps = []
        for d in range(1, nl):
            src = z_out.at[c]
            if pieces > 1:
                src = z_out.at[c, pl.ds(pl.multiple_of(loop_at(d) * prow, prow), prow)]
            cps.append(send(src, z_in.at[c, l], zr_sem.at[c, d - 1], w, loop_at(d)))
        zr_cp.append(cps)
        if pieces > 1:
            z_in[c, l] = z_out[c, pl.ds(pl.multiple_of(l * prow, prow), prow), :]
        else:
            z_in[c, l] = z_out[c]

    def piece(which, d):
        at = loop_at(-d) * prow if pieces > 1 else 0
        return core * nch + which, pl.ds(pl.multiple_of(at, prow), prow)

    za_cp, ap_cp, as_cp = [], [], []

    def to_plane(c, d):
        who, rws = piece(chip, d)
        ref = out_grads.at[who, rws, gcols(c)]
        cps = [send(ref, ref, ap_sem.at[c, d, e - 1], chip_at(e) * 2 + core, l)
               for e in range(1, nch)]
        as_cp.append(send(ref, ref, as_sem.at[c, d, 0], sib, l))
        return cps

    for c in range(G_CHUNKS):
        for cp in zr_cp[c]:
            cp.wait_recv()
        acc = z_in[c, 0].astype(f32)
        for k in range(1, nl):
            acc = acc + z_in[c, k].astype(f32)
        who, rws = piece(chip, 0)
        out_grads[who, rws, gcols(c)] = acc.astype(bf16)
        ref = out_grads.at[who, rws, gcols(c)]
        if pieces > 1:
            za_cp.append([send(ref, ref, za_sem.at[c, d - 1], w, loop_at(d))
                          for d in range(1, nl)])
        ap_cp.append([to_plane(c, 0)])
    for d in range(1, pieces):
        for c in range(G_CHUNKS):
            za_cp[c][d - 1].wait_recv()
            ap_cp[c].append(to_plane(c, d))
    for d in range(pieces):
        for c in range(G_CHUNKS):
            for e in range(1, nch):
                ap_cp[c][d][e - 1].wait_recv()
                who, rws = piece(chip_at(-e), d)
                ref = out_grads.at[who, rws, gcols(c)]
                as_cp.append(send(ref, ref, as_sem.at[c, d, e], sib, l))

    for cp in lg_cp:
        cp.wait_recv()
    for k in range(nw):
        out_logits[pl.ds(k, 1), :] = lg_buf[k, :1, :]
    for cp in as_cp:
        cp.wait_recv()
    for cp in sent:
        cp.wait_send()
    for on, make in maybe_sent:
        pl.when(on)(functools.partial(lambda make: make().wait_send(), make))


def body(feats, tiles, tile_rows, tile_cols, tile_count, w_msg, w_self, readout, labels):
    rows_dev, width = feats.shape
    tb = tiles.shape[-1]
    ns = tiles.shape[2]
    nw, nl = lax.axis_size("wide"), lax.axis_size("loop")
    nch = nw // 2
    share = rows_dev // nw
    gshare = width // nch
    cw = width // CHUNKS
    gw = width // G_CHUNKS
    prow = gshare // nl
    if prow < 16:
        prow = gshare
    pieces = gshare // prow
    bf16, f32 = jnp.bfloat16, jnp.float32
    sends = (
        CHUNKS * (nch + 1) + G_CHUNKS * nch + nw - 1 + 2 * G_CHUNKS * (nl - 1)
        + G_CHUNKS * pieces * (2 * nch - 1)
    )
    vmem = pl.BlockSpec(memory_space=pltpu.VMEM)
    hbm = pl.BlockSpec(memory_space=pltpu.HBM)
    dma = pltpu.SemaphoreType.DMA
    logits, grads = pl.pallas_call(
        functools.partial(kernel, nl, nw, ns, tb),
        out_shape=(
            jax.ShapeDtypeStruct((nw, share), f32),
            jax.ShapeDtypeStruct((nw, gshare, width), bf16),
        ),
        in_specs=[hbm] * 9,
        out_specs=(vmem, vmem),
        scratch_shapes=[
            pltpu.SMEM((ns,), jnp.int32),
            pltpu.SMEM((ns,), jnp.int32),
            pltpu.SMEM((1,), jnp.int32),
            pltpu.VMEM((1, width), f32),
            pltpu.VMEM((nw, share), jnp.int32),
            pltpu.VMEM((CHUNKS, nl * tb, cw), bf16),
            pltpu.VMEM((ns, tb, tb), bf16),
            pltpu.VMEM((2 * share, width), bf16),
            pltpu.VMEM((2 * share, width), bf16),
            pltpu.VMEM((G_CHUNKS, 2 * share, gw), bf16),
            pltpu.VMEM((width, width), bf16),
            pltpu.VMEM((width, width), bf16),
            pltpu.VMEM((2, nch * share, nl * tb), bf16),
            pltpu.VMEM((CHUNKS, 2, nch * share, cw), bf16),
            pltpu.VMEM((CHUNKS, nch * share, cw), bf16),
            pltpu.VMEM((CHUNKS, nch * share, cw), bf16),
            pltpu.VMEM((CHUNKS, nch - 1, share, cw), bf16),
            pltpu.VMEM((share, width), f32),
            pltpu.VMEM((width, 2 * share), bf16),
            pltpu.VMEM((G_CHUNKS, nch * gshare, gw), bf16),
            pltpu.VMEM((G_CHUNKS, nch - 1, gshare, gw), bf16),
            pltpu.VMEM((G_CHUNKS, gshare, gw), bf16),
            pltpu.VMEM((G_CHUNKS, nl, prow, gw), bf16),
            pltpu.VMEM((nw, 8, share), f32),
            dma((9 + CHUNKS,)),
            dma((sends,)),
            dma((CHUNKS, nl - 1)),
            dma((CHUNKS, nl - 1)),
            dma((CHUNKS, nl - 1)),
            dma((CHUNKS, nl - 1)),
            dma((CHUNKS,)),
            dma((CHUNKS, nch - 1)),
            dma((CHUNKS,)),
            dma((G_CHUNKS,)),
            dma((G_CHUNKS, nch - 1)),
            dma((G_CHUNKS, nl - 1)),
            dma((G_CHUNKS, nl - 1)),
            dma((G_CHUNKS, pieces, nch - 1)),
            dma((G_CHUNKS, pieces, nch)),
            dma((nw - 1,)),
        ],
        compiler_params=pltpu.CompilerParams(
            collective_id=0, has_side_effects=True
        ),
    )(
        feats, tiles.reshape(ns, tb, tb), tile_rows.reshape(ns), tile_cols.reshape(ns),
        tile_count.reshape(1), w_msg, w_self, readout.reshape(1, width),
        labels.reshape(nw, share),
    )
    both = grads.reshape(2, width, width)
    return logits.reshape(rows_dev), both[0], both[1]


def solution(mesh):
    placed = (
        P("loop", None),
        P("loop", "wide", None, None, None),
        P("loop", "wide", None),
        P("loop", "wide", None),
        P("loop", "wide"),
        P(),
        P(),
        P(),
        P("loop"),
    )
    return jax.shard_map(
        body, mesh=mesh, in_specs=placed, out_specs=(P("loop"), P(), P()), check_vma=False
    )
```

```python
import functools

import jax
import jax.numpy as jnp
from jax import lax
from jax.experimental import pallas as pl
from jax.experimental.pallas import tpu as pltpu
from jax.sharding import PartitionSpec as P

CHUNKS = 4
G_CHUNKS = 4
ROW_STEP = 32


def kernel(
    nl, nw, ns, tb,
    feats, tiles, rows_in, cols_in, count_in, w_msg, w_self, readout_in, labels_in,
    out_logits, out_grads,
    t_rows, t_cols, t_count, readout, labels,
    gath, tiles_v, nf2, msg2, pg2, wm_v, ws_v, adj, part, sib_in, plane_out, plane_in, pre, trans,
    g_out, g_in, z_out, z_in, lg_buf,
    local_sem, send_sem, right_send, left_send, right_sem, left_sem, rs_sib_sem, rs_pl_sem, msg_sem, pg_sem, g_pl_sem, zr_sem, za_sem,
    ap_sem, as_sem, lg_sem,
):
    f32, bf16 = jnp.float32, jnp.bfloat16
    rows_dev, width = feats.shape
    nb = rows_dev // tb
    nch = nw // 2
    share = rows_dev // nw
    gshare = width // nch
    cw = width // CHUNKS
    gw = width // G_CHUNKS
    prow = z_in.shape[2]
    pieces = gshare // prow
    w = lax.axis_index("wide")
    l = lax.axis_index("loop")
    core = lax.rem(w, 2)
    chip = lax.div(w, 2)
    other = 1 - core
    sib = chip * 2 + other

    def cols(c):
        return pl.ds(c * cw, cw)

    def gcols(c):
        return pl.ds(c * gw, gw)

    def block_rows(q):
        return pl.ds(pl.multiple_of(q * tb, tb), tb)

    locs = [
        pltpu.make_async_copy(tiles, tiles_v, local_sem.at[0]),
        pltpu.make_async_copy(
            feats.at[pl.ds(pl.multiple_of(chip * 2 * share, 2 * share), 2 * share)], nf2,
            local_sem.at[1],
        ),
        pltpu.make_async_copy(w_self, ws_v, local_sem.at[2]),
        pltpu.make_async_copy(w_msg, wm_v, local_sem.at[3]),
        pltpu.make_async_copy(rows_in, t_rows, local_sem.at[4]),
        pltpu.make_async_copy(cols_in, t_cols, local_sem.at[5]),
        pltpu.make_async_copy(readout_in, readout, local_sem.at[6]),
        pltpu.make_async_copy(labels_in, labels, local_sem.at[7]),
        pltpu.make_async_copy(count_in, t_count, local_sem.at[8]),
    ]
    own_rows = pl.ds(pl.multiple_of(lax.rem(w, nb) * tb, tb), tb)
    own_copies = []
    for c in range(CHUNKS):
        own_copies.append(pltpu.make_async_copy(
            feats.at[own_rows, cols(c)],
            gath.at[c, block_rows(l)],
            local_sem.at[9 + c],
        ))
    for cp in locs + own_copies:
        cp.start()

    barrier = pltpu.get_barrier_semaphore()
    for d in range(1, nw):
        pl.semaphore_signal(barrier, inc=1, device_id={"wide": lax.rem(w + d, nw), "loop": l},
                            device_id_type=pl.DeviceIdType.MESH)
    for d in range(1, nl):
        pl.semaphore_signal(barrier, inc=1, device_id={"wide": w, "loop": lax.rem(l + d, nl)},
                            device_id_type=pl.DeviceIdType.MESH)
    pl.semaphore_wait(barrier, nw + nl - 2)

    sent = []

    def send(src, dst, recv, wide, loop):
        cp = pltpu.make_async_remote_copy(
            src_ref=src, dst_ref=dst, send_sem=send_sem.at[len(sent)], recv_sem=recv,
            device_id={"wide": wide, "loop": loop}, device_id_type=pl.DeviceIdType.MESH,
        )
        cp.start()
        sent.append(cp)
        return cp

    def chip_at(e):
        return lax.rem(chip + e + nch, nch)

    def loop_at(d):
        return lax.rem(l + d + nl, nl)

    maybe_sent = []

    def send_if(on, src, c, block, dist, to_right, step):
        send_s = (right_send if to_right else left_send).at[c, dist - 1]
        recv_s = (right_sem if to_right else left_sem).at[c, dist - 1]

        def make():
            return pltpu.make_async_remote_copy(
                src_ref=src(), dst_ref=gath.at[c, block_rows(block)], send_sem=send_s, recv_sem=recv_s,
                device_id={"wide": w, "loop": l + step if to_right else l - step},
                device_id_type=pl.DeviceIdType.MESH,
            )

        @pl.when(on)
        def _():
            make().start()

        maybe_sent.append((on, make))

    def wait_if(on, c, dist, from_left):
        @pl.when(on)
        def _():
            ref = gath.at[c, block_rows(l - dist if from_left else l + dist)]
            pltpu.make_async_remote_copy(
                src_ref=ref, dst_ref=ref, send_sem=send_sem.at[0],
                recv_sem=(right_sem if from_left else left_sem).at[c, dist - 1],
                device_id={"wide": w, "loop": l - 1 if from_left else l + 1},
                device_id_type=pl.DeviceIdType.MESH,
            ).wait_recv()

    relayed = range(2, nl - 1)
    for c in range(CHUNKS):
        for d in (2, 1):
            if d < nl:
                own = functools.partial(lambda c: feats.at[own_rows, cols(c)], c)
                send_if(l + d < nl, own, c, l, d, True, d)
                send_if(l >= d, own, c, l, d, False, d)

    def relay(c):
        for t in relayed:
            wait_if(l >= t, c, t, True)
            send_if(jnp.logical_and(l >= t, l + 1 < nl),
                    functools.partial(lambda c, t: gath.at[c, block_rows(l - t)], c, t),
                    c, l - t, t + 1, True, 1)
            wait_if(l + t < nl, c, t, False)
            send_if(jnp.logical_and(l + t < nl, l >= 1),
                    functools.partial(lambda c, t: gath.at[c, block_rows(l + t)], c, t),
                    c, l + t, t + 1, False, 1)

    def gathered(c):
        own_copies[c].wait()
        for t in range(1, nl):
            if t not in relayed:
                wait_if(l >= t, c, t, True)
                wait_if(l + t < nl, c, t, False)

    for k in (0, 4, 5, 8):
        locs[k].wait()
    cell = [
        jnp.where(s < t_count[0], t_rows[s] * nl + t_cols[s], -1) for s in range(ns)
    ]
    group = 4
    steps = tb // ROW_STEP

    def densify(i, carry):
        r = lax.div(i, steps)
        h = lax.rem(i, steps)
        first = r * tb + h * ROW_STEP
        share_id = lax.div(first, share)
        at = lax.div(share_id, 2) * share + lax.rem(first, share)
        for q0 in range(0, nl, group):
            accs = [jnp.zeros((ROW_STEP, tb), f32) for _ in range(group)]
            for s in range(ns):
                t = tiles_v[s, pl.ds(pl.multiple_of(h * ROW_STEP, ROW_STEP), ROW_STEP), :].astype(f32)
                for g in range(group):
                    on = jnp.where(cell[s] == r * nl + q0 + g, 1.0, 0.0).astype(f32)
                    accs[g] = accs[g] + on * t
            for g in range(group):
                adj[lax.rem(share_id, 2), pl.ds(pl.multiple_of(at, ROW_STEP), ROW_STEP),
                    pl.ds((q0 + g) * tb, tb)] = accs[g].astype(bf16)
        return carry

    lax.fori_loop(0, nb * steps // 2, densify, 0)
    relay(0)
    lax.fori_loop(nb * steps // 2, nb * steps, densify, 0)
    relay(1)

    sib_cp, pl_cp = [], []

    def partial_of(c):
        gathered(c)
        part[c, other] = jnp.dot(adj[other], gath[c], preferred_element_type=f32).astype(bf16)
        sib_cp.append(send(part.at[c, other], sib_in.at[c], rs_sib_sem.at[c], sib, l))
        part[c, core] = jnp.dot(adj[core], gath[c], preferred_element_type=f32).astype(bf16)

    def pair_sum(c, mine, theirs, out):
        out[c] = (mine[c, core].astype(f32) + theirs[c].astype(f32)).astype(bf16)

    def spread(c, out, land, sems, size):
        return [
            send(out.at[c, pl.ds(pl.multiple_of(chip_at(e) * size, size), size)],
                 land.at[c, e - 1], sems.at[c, e - 1], chip_at(e) * 2 + core, l)
            for e in range(1, nch)
        ]

    def total(c, out, land, size):
        acc = out[c, pl.ds(pl.multiple_of(chip * size, size), size), :].astype(f32)
        for e in range(1, nch):
            acc = acc + land[c, e - 1].astype(f32)
        return acc

    def to_chips(c):
        sib_cp[c].wait_recv()
        pair_sum(c, part, sib_in, plane_out)
        pl_cp.append(spread(c, plane_out, plane_in, rs_pl_sem, share))

    partial_of(0)
    for c in range(2, CHUNKS):
        relay(c)
        partial_of(c - 1)
        to_chips(c - 2)
    partial_of(CHUNKS - 1)
    to_chips(CHUNKS - 2)
    to_chips(CHUNKS - 1)

    for k in (1, 2, 3, 6, 7):
        locs[k].wait()
    mine = pl.ds(pl.multiple_of(core * share, share), share)
    nf = nf2[mine, :]
    pre[...] = jnp.dot(nf, ws_v[...], preferred_element_type=f32)

    @pl.when(core == 1)
    def _():
        trans[...] = nf2[...].astype(f32).T.astype(bf16)

    label_col = jnp.broadcast_to(
        labels[pl.ds(w, 1), :].astype(f32), (128, share)).T[:, :1]

    msg_cp = []
    for c in range(CHUNKS):
        for cp in pl_cp[c]:
            cp.wait_recv()
        msg = total(c, plane_out, plane_in, share).astype(bf16)
        pre[...] += jnp.dot(msg, wm_v[pl.ds(c * cw, cw), :], preferred_element_type=f32)
        msg2[mine, cols(c)] = msg
        ref = msg2.at[mine, cols(c)]
        msg_cp.append(send(ref, ref, msg_sem.at[c], sib, l))

    act = pre[...]
    gate = jax.nn.sigmoid(act)
    ro = readout[...]
    hidden = nf.astype(f32) + act * gate
    logit = jnp.sum(hidden * ro, axis=1, keepdims=True)
    resid = jax.nn.sigmoid(logit) - label_col
    pg = (resid * ro * gate * (1.0 + act * (1.0 - gate))).astype(bf16)

    pg_cp = []
    for c in range(G_CHUNKS):
        pg2[c, mine, :] = pg[:, c * gw:(c + 1) * gw]
        ref = pg2.at[c, mine]
        pg_cp.append(send(ref, ref, pg_sem.at[c], sib, l))
    for cp in msg_cp:
        cp.wait_recv()

    @pl.when(core == 0)
    def _():
        trans[...] = msg2[...].astype(f32).T.astype(bf16)

    pl_cp = []
    for c in range(G_CHUNKS):
        pg_cp[c].wait_recv()
        g_out[c] = jnp.dot(trans[...], pg2[c], preferred_element_type=f32).astype(bf16)
        pl_cp.append(spread(c, g_out, g_in, g_pl_sem, gshare))
    lg_buf[w] = jnp.broadcast_to(logit, (share, 128)).T[:8, :]
    lg_cp = [send(lg_buf.at[w], lg_buf.at[w], lg_sem.at[d - 1], lax.rem(w + d, nw), l)
             for d in range(1, nw)]

    zr_cp, za_cp, ap_cp, as_cp = [], [], [], []

    def loop_reduce(c):
        for cp in pl_cp[c]:
            cp.wait_recv()
        z_out[c] = total(c, g_out, g_in, gshare).astype(bf16)
        cps = []
        for d in range(1, nl):
            src = z_out.at[c]
            if pieces > 1:
                src = z_out.at[c, pl.ds(pl.multiple_of(loop_at(d) * prow, prow), prow)]
            cps.append(send(src, z_in.at[c, l], zr_sem.at[c, d - 1], w, loop_at(d)))
        zr_cp.append(cps)
        if pieces > 1:
            z_in[c, l] = z_out[c, pl.ds(pl.multiple_of(l * prow, prow), prow), :]
        else:
            z_in[c, l] = z_out[c]

    def loop_gather(c):
        for cp in zr_cp[c]:
            cp.wait_recv()
        acc = z_in[c, 0].astype(f32)
        for k in range(1, nl):
            acc = acc + z_in[c, k].astype(f32)
        at = l * prow if pieces > 1 else 0
        rws = pl.ds(pl.multiple_of(at, prow), prow)
        out_grads[core * nch + chip, rws, gcols(c)] = acc.astype(bf16)
        ref = out_grads.at[core * nch + chip, rws, gcols(c)]
        za_cp.append([send(ref, ref, za_sem.at[c, d - 1], w, loop_at(d))
                      for d in range(1, nl)] if pieces > 1 else [])

    def chip_gather(c):
        for cp in za_cp[c]:
            cp.wait_recv()
        ref = out_grads.at[core * nch + chip, :, gcols(c)]
        ap_cp.append([send(ref, ref, ap_sem.at[c, e - 1], chip_at(e) * 2 + core, l)
                      for e in range(1, nch)])
        as_cp.append(send(ref, ref, as_sem.at[c, 0], sib, l))

    def core_gather(c):
        for e in range(1, nch):
            ap_cp[c][e - 1].wait_recv()
            ref = out_grads.at[core * nch + chip_at(-e), :, gcols(c)]
            as_cp.append(send(ref, ref, as_sem.at[c, e], sib, l))

    for i in range(G_CHUNKS + 4):
        for stage, late in ((loop_reduce, 0), (loop_gather, 1), (chip_gather, 2), (core_gather, 4)):
            if 0 <= i - late < G_CHUNKS:
                stage(i - late)

    for cp in lg_cp:
        cp.wait_recv()
    for k in range(nw):
        out_logits[pl.ds(k, 1), :] = lg_buf[k, :1, :]
    for cp in as_cp:
        cp.wait_recv()
    for cp in sent:
        cp.wait_send()
    for on, make in maybe_sent:
        pl.when(on)(functools.partial(lambda make: make().wait_send(), make))


def body(feats, tiles, tile_rows, tile_cols, tile_count, w_msg, w_self, readout, labels):
    rows_dev, width = feats.shape
    tb = tiles.shape[-1]
    ns = tiles.shape[2]
    nw, nl = lax.axis_size("wide"), lax.axis_size("loop")
    nch = nw // 2
    share = rows_dev // nw
    gshare = width // nch
    cw = width // CHUNKS
    gw = width // G_CHUNKS
    prow = gshare // nl
    if prow < 16:
        prow = gshare
    bf16, f32 = jnp.bfloat16, jnp.float32
    sends = (
        CHUNKS * (nch + 1) + G_CHUNKS * nch + nw - 1 + 2 * G_CHUNKS * (nl - 1)
        + G_CHUNKS * (2 * nch - 1)
    )
    vmem = pl.BlockSpec(memory_space=pltpu.VMEM)
    hbm = pl.BlockSpec(memory_space=pltpu.HBM)
    dma = pltpu.SemaphoreType.DMA
    logits, grads = pl.pallas_call(
        functools.partial(kernel, nl, nw, ns, tb),
        out_shape=(
            pltpu.VMEM((nw, share), f32),
            pltpu.VMEM((nw, gshare, width), bf16),
        ),
        in_specs=[hbm] * 9,
        out_specs=(vmem, vmem),
        scratch_shapes=[
            pltpu.SMEM((ns,), jnp.int32),
            pltpu.SMEM((ns,), jnp.int32),
            pltpu.SMEM((1,), jnp.int32),
            pltpu.VMEM((1, width), f32),
            pltpu.VMEM((nw, share), jnp.int32),
            pltpu.VMEM((CHUNKS, nl * tb, cw), bf16),
            pltpu.VMEM((ns, tb, tb), bf16),
            pltpu.VMEM((2 * share, width), bf16),
            pltpu.VMEM((2 * share, width), bf16),
            pltpu.VMEM((G_CHUNKS, 2 * share, gw), bf16),
            pltpu.VMEM((width, width), bf16),
            pltpu.VMEM((width, width), bf16),
            pltpu.VMEM((2, nch * share, nl * tb), bf16),
            pltpu.VMEM((CHUNKS, 2, nch * share, cw), bf16),
            pltpu.VMEM((CHUNKS, nch * share, cw), bf16),
            pltpu.VMEM((CHUNKS, nch * share, cw), bf16),
            pltpu.VMEM((CHUNKS, nch - 1, share, cw), bf16),
            pltpu.VMEM((share, width), f32),
            pltpu.VMEM((width, 2 * share), bf16),
            pltpu.VMEM((G_CHUNKS, nch * gshare, gw), bf16),
            pltpu.VMEM((G_CHUNKS, nch - 1, gshare, gw), bf16),
            pltpu.VMEM((G_CHUNKS, gshare, gw), bf16),
            pltpu.VMEM((G_CHUNKS, nl, prow, gw), bf16),
            pltpu.VMEM((nw, 8, share), f32),
            dma((9 + CHUNKS,)),
            dma((sends,)),
            dma((CHUNKS, nl - 1)),
            dma((CHUNKS, nl - 1)),
            dma((CHUNKS, nl - 1)),
            dma((CHUNKS, nl - 1)),
            dma((CHUNKS,)),
            dma((CHUNKS, nch - 1)),
            dma((CHUNKS,)),
            dma((G_CHUNKS,)),
            dma((G_CHUNKS, nch - 1)),
            dma((G_CHUNKS, nl - 1)),
            dma((G_CHUNKS, nl - 1)),
            dma((G_CHUNKS, nch - 1)),
            dma((G_CHUNKS, nch)),
            dma((nw - 1,)),
        ],
        compiler_params=pltpu.CompilerParams(
            collective_id=0, has_side_effects=True, vmem_limit_bytes=60 * 2**20
        ),
    )(
        feats, tiles.reshape(ns, tb, tb), tile_rows.reshape(ns), tile_cols.reshape(ns),
        tile_count.reshape(1), w_msg, w_self, readout.reshape(1, width),
        labels.reshape(nw, share),
    )
    both = grads.reshape(2, width, width)
    return logits.reshape(rows_dev), both[0], both[1]


def solution(mesh):
    placed = (
        P("loop", None),
        P("loop", "wide", None, None, None),
        P("loop", "wide", None),
        P("loop", "wide", None),
        P("loop", "wide"),
        P(),
        P(),
        P(),
        P("loop"),
    )
    return jax.shard_map(
        body, mesh=mesh, in_specs=placed, out_specs=(P("loop"), P(), P()), check_vma=False
    )
```

```python
import functools

import jax
import jax.numpy as jnp
from jax import lax
from jax.experimental import pallas as pl
from jax.experimental.pallas import tpu as pltpu
from jax.sharding import PartitionSpec as P

CHUNKS = 4
G_CHUNKS = 2
ROW_STEP = 32


def kernel(
    nl, nw, ns, tb,
    feats, tiles, rows_in, cols_in, count_in, w_msg, w_self, readout_in, labels_in,
    out_logits, out_grads,
    t_rows, t_cols, t_count, readout, labels,
    gath, tiles_v, nf2, msg2, pg2, wm_v, ws_v, adj, part, sib_in, plane_out, plane_in, pre, trans,
    g_out, g_in, z_out, z_in, lg_buf,
    local_sem, send_sem, right_send, left_send, right_sem, left_sem, rs_sib_sem, rs_pl_sem, msg_sem, pg_sem, g_pl_sem, zr_sem, za_sem,
    ap_sem, as_sem, lg_sem,
):
    f32, bf16 = jnp.float32, jnp.bfloat16
    rows_dev, width = feats.shape
    nb = rows_dev // tb
    nch = nw // 2
    share = rows_dev // nw
    gshare = width // nch
    cw = width // CHUNKS
    crow = gshare // G_CHUNKS
    prow = z_in.shape[2]
    pieces = crow // prow
    w = lax.axis_index("wide")
    l = lax.axis_index("loop")
    core = lax.rem(w, 2)
    chip = lax.div(w, 2)
    other = 1 - core
    sib = chip * 2 + other

    def cols(c):
        return pl.ds(c * cw, cw)

    def block_rows(q):
        return pl.ds(pl.multiple_of(q * tb, tb), tb)

    locs = [
        pltpu.make_async_copy(tiles, tiles_v, local_sem.at[0]),
        pltpu.make_async_copy(
            feats.at[pl.ds(pl.multiple_of(chip * 2 * share, 2 * share), 2 * share)], nf2,
            local_sem.at[1],
        ),
        pltpu.make_async_copy(w_self, ws_v, local_sem.at[2]),
        pltpu.make_async_copy(w_msg, wm_v, local_sem.at[3]),
        pltpu.make_async_copy(rows_in, t_rows, local_sem.at[4]),
        pltpu.make_async_copy(cols_in, t_cols, local_sem.at[5]),
        pltpu.make_async_copy(readout_in, readout, local_sem.at[6]),
        pltpu.make_async_copy(labels_in, labels, local_sem.at[7]),
        pltpu.make_async_copy(count_in, t_count, local_sem.at[8]),
    ]
    own_rows = pl.ds(pl.multiple_of(lax.rem(w, nb) * tb, tb), tb)
    own_copies = []
    for c in range(CHUNKS):
        own_copies.append(pltpu.make_async_copy(
            feats.at[own_rows, cols(c)],
            gath.at[c, block_rows(l)],
            local_sem.at[9 + c],
        ))
    for cp in locs + own_copies:
        cp.start()

    barrier = pltpu.get_barrier_semaphore()
    for d in range(1, nw):
        pl.semaphore_signal(barrier, inc=1, device_id={"wide": lax.rem(w + d, nw), "loop": l},
                            device_id_type=pl.DeviceIdType.MESH)
    for d in range(1, nl):
        pl.semaphore_signal(barrier, inc=1, device_id={"wide": w, "loop": lax.rem(l + d, nl)},
                            device_id_type=pl.DeviceIdType.MESH)
    pl.semaphore_wait(barrier, nw + nl - 2)

    sent = []

    def send(src, dst, recv, wide, loop):
        cp = pltpu.make_async_remote_copy(
            src_ref=src, dst_ref=dst, send_sem=send_sem.at[len(sent)], recv_sem=recv,
            device_id={"wide": wide, "loop": loop}, device_id_type=pl.DeviceIdType.MESH,
        )
        cp.start()
        sent.append(cp)
        return cp

    def chip_at(e):
        return lax.rem(chip + e + nch, nch)

    def loop_at(d):
        return lax.rem(l + d + nl, nl)

    maybe_sent = []

    def send_if(on, src, c, block, dist, to_right, step):
        send_s = (right_send if to_right else left_send).at[c, dist - 1]
        recv_s = (right_sem if to_right else left_sem).at[c, dist - 1]

        def make():
            return pltpu.make_async_remote_copy(
                src_ref=src(), dst_ref=gath.at[c, block_rows(block)], send_sem=send_s, recv_sem=recv_s,
                device_id={"wide": w, "loop": l + step if to_right else l - step},
                device_id_type=pl.DeviceIdType.MESH,
            )

        @pl.when(on)
        def _():
            make().start()

        maybe_sent.append((on, make))

    def wait_if(on, c, dist, from_left):
        @pl.when(on)
        def _():
            ref = gath.at[c, block_rows(l - dist if from_left else l + dist)]
            pltpu.make_async_remote_copy(
                src_ref=ref, dst_ref=ref, send_sem=send_sem.at[0],
                recv_sem=(right_sem if from_left else left_sem).at[c, dist - 1],
                device_id={"wide": w, "loop": l - 1 if from_left else l + 1},
                device_id_type=pl.DeviceIdType.MESH,
            ).wait_recv()

    relayed = range(2, nl - 1)
    for c in range(CHUNKS):
        for d in (2, 1):
            if d < nl:
                own = functools.partial(lambda c: feats.at[own_rows, cols(c)], c)
                send_if(l + d < nl, own, c, l, d, True, d)
                send_if(l >= d, own, c, l, d, False, d)

    def relay(c):
        for t in relayed:
            wait_if(l >= t, c, t, True)
            send_if(jnp.logical_and(l >= t, l + 1 < nl),
                    functools.partial(lambda c, t: gath.at[c, block_rows(l - t)], c, t),
                    c, l - t, t + 1, True, 1)
            wait_if(l + t < nl, c, t, False)
            send_if(jnp.logical_and(l + t < nl, l >= 1),
                    functools.partial(lambda c, t: gath.at[c, block_rows(l + t)], c, t),
                    c, l + t, t + 1, False, 1)

    def gathered(c):
        own_copies[c].wait()
        for t in range(1, nl):
            if t not in relayed:
                wait_if(l >= t, c, t, True)
                wait_if(l + t < nl, c, t, False)

    for k in (0, 4, 5, 8):
        locs[k].wait()
    cell = [
        jnp.where(s < t_count[0], t_rows[s] * nl + t_cols[s], -1) for s in range(ns)
    ]
    group = 4
    steps = tb // ROW_STEP

    def densify(i, carry):
        r = lax.div(i, steps)
        h = lax.rem(i, steps)
        first = r * tb + h * ROW_STEP
        share_id = lax.div(first, share)
        at = lax.div(share_id, 2) * share + lax.rem(first, share)
        for q0 in range(0, nl, group):
            accs = [jnp.zeros((ROW_STEP, tb), f32) for _ in range(group)]
            for s in range(ns):
                t = tiles_v[s, pl.ds(pl.multiple_of(h * ROW_STEP, ROW_STEP), ROW_STEP), :].astype(f32)
                for g in range(group):
                    on = jnp.where(cell[s] == r * nl + q0 + g, 1.0, 0.0).astype(f32)
                    accs[g] = accs[g] + on * t
            for g in range(group):
                adj[lax.rem(share_id, 2), pl.ds(pl.multiple_of(at, ROW_STEP), ROW_STEP),
                    pl.ds((q0 + g) * tb, tb)] = accs[g].astype(bf16)
        return carry

    lax.fori_loop(0, nb * steps // 2, densify, 0)
    relay(0)
    lax.fori_loop(nb * steps // 2, nb * steps, densify, 0)
    relay(1)

    sib_cp, pl_cp = [], []

    def partial_of(c):
        gathered(c)
        part[c, other] = jnp.dot(adj[other], gath[c], preferred_element_type=f32).astype(bf16)
        sib_cp.append(send(part.at[c, other], sib_in.at[c], rs_sib_sem.at[c], sib, l))
        part[c, core] = jnp.dot(adj[core], gath[c], preferred_element_type=f32).astype(bf16)

    def pair_sum(c, mine, theirs, out):
        out[c] = (mine[c, core].astype(f32) + theirs[c].astype(f32)).astype(bf16)

    def spread(c, out, land, sems, size):
        return [
            send(out.at[c, pl.ds(pl.multiple_of(chip_at(e) * size, size), size)],
                 land.at[c, e - 1], sems.at[c, e - 1], chip_at(e) * 2 + core, l)
            for e in range(1, nch)
        ]

    def total(c, out, land, size):
        acc = out[c, pl.ds(pl.multiple_of(chip * size, size), size), :].astype(f32)
        for e in range(1, nch):
            acc = acc + land[c, e - 1].astype(f32)
        return acc

    def to_chips(c):
        sib_cp[c].wait_recv()
        pair_sum(c, part, sib_in, plane_out)
        pl_cp.append(spread(c, plane_out, plane_in, rs_pl_sem, share))

    partial_of(0)
    for c in range(2, CHUNKS):
        relay(c)
        partial_of(c - 1)
        to_chips(c - 2)
    partial_of(CHUNKS - 1)
    to_chips(CHUNKS - 2)
    to_chips(CHUNKS - 1)

    for k in (1, 2, 3, 6, 7):
        locs[k].wait()
    mine = pl.ds(pl.multiple_of(core * share, share), share)
    nf = nf2[mine, :]
    pre[...] = jnp.dot(nf, ws_v[...], preferred_element_type=f32)

    def put_trans(first, block):
        for j in range(block.shape[0] // crow):
            k, at = divmod(first + j * crow, gshare)
            trans[at // crow, pl.ds(k * crow, crow), :] = block[j * crow:(j + 1) * crow]

    def msg_trans(c):
        msg_cp[c].wait_recv()

        @pl.when(core == 0)
        def _():
            put_trans(c * cw, msg2[:, cols(c)].astype(f32).T.astype(bf16))

    @pl.when(core == 1)
    def _():
        put_trans(0, nf2[...].astype(f32).T.astype(bf16))

    label_col = jnp.broadcast_to(
        labels[pl.ds(w, 1), :].astype(f32), (128, share)).T[:, :1]

    msg_cp = []
    for c in range(CHUNKS):
        for cp in pl_cp[c]:
            cp.wait_recv()
        msg = total(c, plane_out, plane_in, share).astype(bf16)
        pre[...] += jnp.dot(msg, wm_v[pl.ds(c * cw, cw), :], preferred_element_type=f32)
        msg2[mine, cols(c)] = msg
        ref = msg2.at[mine, cols(c)]
        msg_cp.append(send(ref, ref, msg_sem.at[c], sib, l))
        if c > 0:
            msg_trans(c - 1)

    act = pre[...]
    gate = jax.nn.sigmoid(act)
    ro = readout[...]
    hidden = nf.astype(f32) + act * gate
    logit = jnp.sum(hidden * ro, axis=1, keepdims=True)
    resid = jax.nn.sigmoid(logit) - label_col
    pg = (resid * ro * gate * (1.0 + act * (1.0 - gate))).astype(bf16)

    pg2[mine, :] = pg
    ref = pg2.at[mine]
    pg_cp = send(ref, ref, pg_sem.at[0], sib, l)
    msg_trans(CHUNKS - 1)
    pg_cp.wait_recv()

    pl_cp = []
    for c in range(G_CHUNKS):
        g_out[c] = jnp.dot(trans[c], pg2[...], preferred_element_type=f32).astype(bf16)
        pl_cp.append(spread(c, g_out, g_in, g_pl_sem, crow))
    lg_buf[w] = jnp.broadcast_to(logit, (share, 128)).T[:8, :]
    lg_cp = [send(lg_buf.at[w], lg_buf.at[w], lg_sem.at[d - 1], lax.rem(w + d, nw), l)
             for d in range(1, nw)]

    zr_cp, za_cp, ap_cp, as_cp = [], [], [], []

    def loop_reduce(c):
        for cp in pl_cp[c]:
            cp.wait_recv()
        z_out[c] = total(c, g_out, g_in, crow).astype(bf16)
        cps = []
        for d in range(1, nl):
            src = z_out.at[c]
            if pieces > 1:
                src = z_out.at[c, pl.ds(pl.multiple_of(loop_at(d) * prow, prow), prow)]
            cps.append(send(src, z_in.at[c, l], zr_sem.at[c, d - 1], w, loop_at(d)))
        zr_cp.append(cps)
        if pieces > 1:
            z_in[c, l] = z_out[c, pl.ds(pl.multiple_of(l * prow, prow), prow), :]
        else:
            z_in[c, l] = z_out[c]

    def loop_gather(c):
        for cp in zr_cp[c]:
            cp.wait_recv()
        acc = z_in[c, 0].astype(f32)
        for k in range(1, nl):
            acc = acc + z_in[c, k].astype(f32)
        at = l * prow if pieces > 1 else 0
        rws = pl.ds(pl.multiple_of(c * crow + at, prow), prow)
        out_grads[core * nch + chip, rws, :] = acc.astype(bf16)
        ref = out_grads.at[core * nch + chip, rws]
        za_cp.append([send(ref, ref, za_sem.at[c, d - 1], w, loop_at(d))
                      for d in range(1, nl)] if pieces > 1 else [])

    def chip_gather(c):
        for cp in za_cp[c]:
            cp.wait_recv()
        ref = out_grads.at[core * nch + chip, pl.ds(c * crow, crow)]
        ap_cp.append([send(ref, ref, ap_sem.at[c, e - 1], chip_at(e) * 2 + core, l)
                      for e in range(1, nch)])
        as_cp.append(send(ref, ref, as_sem.at[c, 0], sib, l))

    def core_gather(c):
        for e in range(1, nch):
            ap_cp[c][e - 1].wait_recv()
            ref = out_grads.at[core * nch + chip_at(-e), pl.ds(c * crow, crow)]
            as_cp.append(send(ref, ref, as_sem.at[c, e], sib, l))

    for i in range(G_CHUNKS + 4):
        for stage, late in ((loop_reduce, 0), (loop_gather, 1), (chip_gather, 2), (core_gather, 4)):
            if 0 <= i - late < G_CHUNKS:
                stage(i - late)

    for cp in lg_cp:
        cp.wait_recv()
    for k in range(nw):
        out_logits[pl.ds(k, 1), :] = lg_buf[k, :1, :]
    for cp in as_cp:
        cp.wait_recv()
    for cp in sent:
        cp.wait_send()
    for on, make in maybe_sent:
        pl.when(on)(functools.partial(lambda make: make().wait_send(), make))


def body(feats, tiles, tile_rows, tile_cols, tile_count, w_msg, w_self, readout, labels):
    rows_dev, width = feats.shape
    tb = tiles.shape[-1]
    ns = tiles.shape[2]
    nw, nl = lax.axis_size("wide"), lax.axis_size("loop")
    nch = nw // 2
    share = rows_dev // nw
    gshare = width // nch
    cw = width // CHUNKS
    crow = gshare // G_CHUNKS
    prow = crow // nl
    if prow < 16:
        prow = crow
    bf16, f32 = jnp.bfloat16, jnp.float32
    sends = (
        CHUNKS * (nch + 1) + 1 + G_CHUNKS * (nch - 1) + nw - 1 + 2 * G_CHUNKS * (nl - 1)
        + G_CHUNKS * (2 * nch - 1)
    )
    vmem = pl.BlockSpec(memory_space=pltpu.VMEM)
    hbm = pl.BlockSpec(memory_space=pltpu.HBM)
    dma = pltpu.SemaphoreType.DMA
    logits, grads = pl.pallas_call(
        functools.partial(kernel, nl, nw, ns, tb),
        out_shape=(
            pltpu.VMEM((nw, share), f32),
            pltpu.VMEM((nw, gshare, width), bf16),
        ),
        in_specs=[hbm] * 9,
        out_specs=(vmem, vmem),
        scratch_shapes=[
            pltpu.SMEM((ns,), jnp.int32),
            pltpu.SMEM((ns,), jnp.int32),
            pltpu.SMEM((1,), jnp.int32),
            pltpu.VMEM((1, width), f32),
            pltpu.VMEM((nw, share), jnp.int32),
            pltpu.VMEM((CHUNKS, nl * tb, cw), bf16),
            pltpu.VMEM((ns, tb, tb), bf16),
            pltpu.VMEM((2 * share, width), bf16),
            pltpu.VMEM((2 * share, width), bf16),
            pltpu.VMEM((2 * share, width), bf16),
            pltpu.VMEM((width, width), bf16),
            pltpu.VMEM((width, width), bf16),
            pltpu.VMEM((2, nch * share, nl * tb), bf16),
            pltpu.VMEM((CHUNKS, 2, nch * share, cw), bf16),
            pltpu.VMEM((CHUNKS, nch * share, cw), bf16),
            pltpu.VMEM((CHUNKS, nch * share, cw), bf16),
            pltpu.VMEM((CHUNKS, nch - 1, share, cw), bf16),
            pltpu.VMEM((share, width), f32),
            pltpu.VMEM((G_CHUNKS, nch * crow, 2 * share), bf16),
            pltpu.VMEM((G_CHUNKS, nch * crow, width), bf16),
            pltpu.VMEM((G_CHUNKS, nch - 1, crow, width), bf16),
            pltpu.VMEM((G_CHUNKS, crow, width), bf16),
            pltpu.VMEM((G_CHUNKS, nl, prow, width), bf16),
            pltpu.VMEM((nw, 8, share), f32),
            dma((9 + CHUNKS,)),
            dma((sends,)),
            dma((CHUNKS, nl - 1)),
            dma((CHUNKS, nl - 1)),
            dma((CHUNKS, nl - 1)),
            dma((CHUNKS, nl - 1)),
            dma((CHUNKS,)),
            dma((CHUNKS, nch - 1)),
            dma((CHUNKS,)),
            dma((1,)),
            dma((G_CHUNKS, nch - 1)),
            dma((G_CHUNKS, nl - 1)),
            dma((G_CHUNKS, nl - 1)),
            dma((G_CHUNKS, nch - 1)),
            dma((G_CHUNKS, nch)),
            dma((nw - 1,)),
        ],
        compiler_params=pltpu.CompilerParams(
            collective_id=0, has_side_effects=True, vmem_limit_bytes=60 * 2**20
        ),
    )(
        feats, tiles.reshape(ns, tb, tb), tile_rows.reshape(ns), tile_cols.reshape(ns),
        tile_count.reshape(1), w_msg, w_self, readout.reshape(1, width),
        labels.reshape(nw, share),
    )
    both = grads.reshape(2, width, width)
    return logits.reshape(rows_dev), both[0], both[1]


def solution(mesh):
    placed = (
        P("loop", None),
        P("loop", "wide", None, None, None),
        P("loop", "wide", None),
        P("loop", "wide", None),
        P("loop", "wide"),
        P(),
        P(),
        P(),
        P("loop"),
    )
    return jax.shard_map(
        body, mesh=mesh, in_specs=placed, out_specs=(P("loop"), P(), P()), check_vma=False
    )
```

```python
import functools

import jax
import jax.numpy as jnp
from jax import lax
from jax.experimental import pallas as pl
from jax.experimental.pallas import tpu as pltpu
from jax.sharding import PartitionSpec as P

CHUNKS = 4
G_CHUNKS = 2
ROW_STEP = 32


def kernel(
    nl, nw, ns, tb,
    feats, tiles, rows_in, cols_in, count_in, w_msg, w_self, readout_in, labels_in,
    out_logits, out_grads,
    t_rows, t_cols, t_count, readout, labels,
    gath, tiles_v, nf2, msg2, pg2, wm_v, ws_v, adj, part, sib_in, plane_out, plane_in, pre, trans,
    g_out, g_in, z_out, z_in, lg_buf,
    local_sem, send_sem, right_send, left_send, right_sem, left_sem, rs_sib_sem, rs_pl_sem, msg_sem, pg_sem, g_pl_sem, zr_sem, za_sem,
    ap_sem, as_sem, lg_sem,
):
    f32, bf16 = jnp.float32, jnp.bfloat16
    rows_dev, width = feats.shape
    nb = rows_dev // tb
    nch = nw // 2
    share = rows_dev // nw
    gshare = width // nch
    cw = width // CHUNKS
    crow = gshare // G_CHUNKS
    prow = z_in.shape[2]
    pieces = crow // prow
    w = lax.axis_index("wide")
    l = lax.axis_index("loop")
    core = lax.rem(w, 2)
    chip = lax.div(w, 2)
    other = 1 - core
    sib = chip * 2 + other

    def cols(c):
        return pl.ds(c * cw, cw)

    def block_rows(q):
        return pl.ds(pl.multiple_of(q * tb, tb), tb)

    locs = [
        pltpu.make_async_copy(tiles, tiles_v, local_sem.at[0]),
        pltpu.make_async_copy(
            feats.at[pl.ds(pl.multiple_of(chip * 2 * share, 2 * share), 2 * share)], nf2,
            local_sem.at[1],
        ),
        pltpu.make_async_copy(w_self, ws_v, local_sem.at[2]),
        pltpu.make_async_copy(w_msg, wm_v, local_sem.at[3]),
        pltpu.make_async_copy(rows_in, t_rows, local_sem.at[4]),
        pltpu.make_async_copy(cols_in, t_cols, local_sem.at[5]),
        pltpu.make_async_copy(readout_in, readout, local_sem.at[6]),
        pltpu.make_async_copy(labels_in, labels, local_sem.at[7]),
        pltpu.make_async_copy(count_in, t_count, local_sem.at[8]),
    ]
    own_rows = pl.ds(pl.multiple_of(lax.rem(w, nb) * tb, tb), tb)
    own_copies = []
    for c in range(CHUNKS):
        own_copies.append(pltpu.make_async_copy(
            feats.at[own_rows, cols(c)],
            gath.at[c, block_rows(l)],
            local_sem.at[9 + c],
        ))
    for cp in own_copies + locs:
        cp.start()

    barrier = pltpu.get_barrier_semaphore()
    for d in range(1, nw):
        pl.semaphore_signal(barrier, inc=1, device_id={"wide": lax.rem(w + d, nw), "loop": l},
                            device_id_type=pl.DeviceIdType.MESH)
    for d in range(1, nl):
        pl.semaphore_signal(barrier, inc=1, device_id={"wide": w, "loop": lax.rem(l + d, nl)},
                            device_id_type=pl.DeviceIdType.MESH)
    pl.semaphore_wait(barrier, nw + nl - 2)

    sent = []

    def send(src, dst, recv, wide, loop):
        cp = pltpu.make_async_remote_copy(
            src_ref=src, dst_ref=dst, send_sem=send_sem.at[len(sent)], recv_sem=recv,
            device_id={"wide": wide, "loop": loop}, device_id_type=pl.DeviceIdType.MESH,
        )
        cp.start()
        sent.append(cp)
        return cp

    def chip_at(e):
        return lax.rem(chip + e + nch, nch)

    def loop_at(d):
        return lax.rem(l + d + nl, nl)

    maybe_sent = []

    def send_if(on, src, c, block, dist, to_right, step):
        send_s = (right_send if to_right else left_send).at[c, dist - 1]
        recv_s = (right_sem if to_right else left_sem).at[c, dist - 1]

        def make():
            return pltpu.make_async_remote_copy(
                src_ref=src(), dst_ref=gath.at[c, block_rows(block)], send_sem=send_s, recv_sem=recv_s,
                device_id={"wide": w, "loop": l + step if to_right else l - step},
                device_id_type=pl.DeviceIdType.MESH,
            )

        @pl.when(on)
        def _():
            make().start()

        maybe_sent.append((on, make))

    def wait_if(on, c, dist, from_left):
        @pl.when(on)
        def _():
            ref = gath.at[c, block_rows(l - dist if from_left else l + dist)]
            pltpu.make_async_remote_copy(
                src_ref=ref, dst_ref=ref, send_sem=send_sem.at[0],
                recv_sem=(right_sem if from_left else left_sem).at[c, dist - 1],
                device_id={"wide": w, "loop": l - 1 if from_left else l + 1},
                device_id_type=pl.DeviceIdType.MESH,
            ).wait_recv()

    relayed = range(2, nl - 1)

    def direct(c):
        own_copies[c].wait()
        own = functools.partial(lambda c: gath.at[c, block_rows(l)], c)
        for d in (2, 1):
            if d < nl:
                send_if(l + d < nl, own, c, l, d, True, d)
                send_if(l >= d, own, c, l, d, False, d)

    for c in range(CHUNKS - 1):
        direct(c)

    def relay(c):
        for t in relayed:
            wait_if(l >= t, c, t, True)
            send_if(jnp.logical_and(l >= t, l + 1 < nl),
                    functools.partial(lambda c, t: gath.at[c, block_rows(l - t)], c, t),
                    c, l - t, t + 1, True, 1)
            wait_if(l + t < nl, c, t, False)
            send_if(jnp.logical_and(l + t < nl, l >= 1),
                    functools.partial(lambda c, t: gath.at[c, block_rows(l + t)], c, t),
                    c, l + t, t + 1, False, 1)

    def gathered(c):
        for t in range(1, nl):
            if t not in relayed:
                wait_if(l >= t, c, t, True)
                wait_if(l + t < nl, c, t, False)

    for k in (0, 4, 5, 8):
        locs[k].wait()
    cell = [
        jnp.where(s < t_count[0], t_rows[s] * nl + t_cols[s], -1) for s in range(ns)
    ]
    group = 4
    steps = tb // ROW_STEP

    def densify(i, carry):
        r = lax.div(i, steps)
        h = lax.rem(i, steps)
        first = r * tb + h * ROW_STEP
        share_id = lax.div(first, share)
        at = lax.div(share_id, 2) * share + lax.rem(first, share)
        for q0 in range(0, nl, group):
            accs = [jnp.zeros((ROW_STEP, tb), f32) for _ in range(group)]
            for s in range(ns):
                t = tiles_v[s, pl.ds(pl.multiple_of(h * ROW_STEP, ROW_STEP), ROW_STEP), :].astype(f32)
                for g in range(group):
                    on = jnp.where(cell[s] == r * nl + q0 + g, 1.0, 0.0).astype(f32)
                    accs[g] = accs[g] + on * t
            for g in range(group):
                adj[lax.rem(share_id, 2), pl.ds(pl.multiple_of(at, ROW_STEP), ROW_STEP),
                    pl.ds((q0 + g) * tb, tb)] = accs[g].astype(bf16)
        return carry

    lax.fori_loop(0, nb * steps // 2, densify, 0)
    relay(0)
    direct(CHUNKS - 1)
    lax.fori_loop(nb * steps // 2, nb * steps, densify, 0)
    relay(1)

    sib_cp, pl_cp = [], []

    def partial_of(c):
        gathered(c)
        part[c, other] = jnp.dot(adj[other], gath[c], preferred_element_type=f32).astype(bf16)
        sib_cp.append(send(part.at[c, other], sib_in.at[c], rs_sib_sem.at[c], sib, l))
        part[c, core] = jnp.dot(adj[core], gath[c], preferred_element_type=f32).astype(bf16)

    def pair_sum(c, mine, theirs, out):
        out[c] = (mine[c, core].astype(f32) + theirs[c].astype(f32)).astype(bf16)

    def spread(c, out, land, sems, size):
        return [
            send(out.at[c, pl.ds(pl.multiple_of(chip_at(e) * size, size), size)],
                 land.at[c, e - 1], sems.at[c, e - 1], chip_at(e) * 2 + core, l)
            for e in range(1, nch)
        ]

    def total(c, out, land, size):
        acc = out[c, pl.ds(pl.multiple_of(chip * size, size), size), :].astype(f32)
        for e in range(1, nch):
            acc = acc + land[c, e - 1].astype(f32)
        return acc

    def to_chips(c):
        sib_cp[c].wait_recv()
        pair_sum(c, part, sib_in, plane_out)
        pl_cp.append(spread(c, plane_out, plane_in, rs_pl_sem, share))

    partial_of(0)
    for c in range(2, CHUNKS):
        relay(c)
        partial_of(c - 1)
        to_chips(c - 2)
    partial_of(CHUNKS - 1)
    to_chips(CHUNKS - 2)
    to_chips(CHUNKS - 1)

    for k in (1, 2, 3, 6, 7):
        locs[k].wait()
    mine = pl.ds(pl.multiple_of(core * share, share), share)
    nf = nf2[mine, :]
    pre[...] = jnp.dot(nf, ws_v[...], preferred_element_type=f32)

    def put_trans(first, block):
        for j in range(block.shape[0] // crow):
            k, at = divmod(first + j * crow, gshare)
            trans[at // crow, pl.ds(k * crow, crow), :] = block[j * crow:(j + 1) * crow]

    def msg_trans(c):
        msg_cp[c].wait_recv()

        @pl.when(core == 0)
        def _():
            put_trans(c * cw, msg2[:, cols(c)].astype(f32).T.astype(bf16))

    @pl.when(core == 1)
    def _():
        put_trans(0, nf2[...].astype(f32).T.astype(bf16))

    label_col = jnp.broadcast_to(
        labels[pl.ds(w, 1), :].astype(f32), (128, share)).T[:, :1]

    msg_cp = []
    for c in range(CHUNKS):
        for cp in pl_cp[c]:
            cp.wait_recv()
        msg = total(c, plane_out, plane_in, share).astype(bf16)
        pre[...] += jnp.dot(msg, wm_v[pl.ds(c * cw, cw), :], preferred_element_type=f32)
        msg2[mine, cols(c)] = msg
        ref = msg2.at[mine, cols(c)]
        msg_cp.append(send(ref, ref, msg_sem.at[c], sib, l))
        if c > 0:
            msg_trans(c - 1)

    act = pre[...]
    gate = jax.nn.sigmoid(act)
    ro = readout[...]
    hidden = nf.astype(f32) + act * gate
    logit = jnp.sum(hidden * ro, axis=1, keepdims=True)
    resid = jax.nn.sigmoid(logit) - label_col
    pg = (resid * ro * gate * (1.0 + act * (1.0 - gate))).astype(bf16)

    pg2[mine, :] = pg
    ref = pg2.at[mine]
    pg_cp = send(ref, ref, pg_sem.at[0], sib, l)
    msg_trans(CHUNKS - 1)
    pg_cp.wait_recv()

    pl_cp = []
    for c in range(G_CHUNKS):
        g_out[c] = jnp.dot(trans[c], pg2[...], preferred_element_type=f32).astype(bf16)
        pl_cp.append(spread(c, g_out, g_in, g_pl_sem, crow))
    lg_buf[w] = jnp.broadcast_to(logit, (share, 128)).T[:8, :]
    lg_cp = [send(lg_buf.at[w], lg_buf.at[w], lg_sem.at[d - 1], lax.rem(w + d, nw), l)
             for d in range(1, nw)]

    zr_cp, za_cp, ap_cp, as_cp = [], [], [], []

    def loop_reduce(c):
        for cp in pl_cp[c]:
            cp.wait_recv()
        z_out[c] = total(c, g_out, g_in, crow).astype(bf16)
        cps = []
        for d in range(1, nl):
            src = z_out.at[c]
            if pieces > 1:
                src = z_out.at[c, pl.ds(pl.multiple_of(loop_at(d) * prow, prow), prow)]
            cps.append(send(src, z_in.at[c, l], zr_sem.at[c, d - 1], w, loop_at(d)))
        zr_cp.append(cps)
        if pieces > 1:
            z_in[c, l] = z_out[c, pl.ds(pl.multiple_of(l * prow, prow), prow), :]
        else:
            z_in[c, l] = z_out[c]

    def loop_gather(c):
        for cp in zr_cp[c]:
            cp.wait_recv()
        acc = z_in[c, 0].astype(f32)
        for k in range(1, nl):
            acc = acc + z_in[c, k].astype(f32)
        at = l * prow if pieces > 1 else 0
        rws = pl.ds(pl.multiple_of(c * crow + at, prow), prow)
        out_grads[core * nch + chip, rws, :] = acc.astype(bf16)
        ref = out_grads.at[core * nch + chip, rws]
        za_cp.append([send(ref, ref, za_sem.at[c, d - 1], w, loop_at(d))
                      for d in range(1, nl)] if pieces > 1 else [])

    def chip_gather(c):
        for cp in za_cp[c]:
            cp.wait_recv()
        ref = out_grads.at[core * nch + chip, pl.ds(c * crow, crow)]
        ap_cp.append([send(ref, ref, ap_sem.at[c, e - 1], chip_at(e) * 2 + core, l)
                      for e in range(1, nch)])
        as_cp.append(send(ref, ref, as_sem.at[c, 0], sib, l))

    def core_gather(c):
        for e in range(1, nch):
            ap_cp[c][e - 1].wait_recv()
            ref = out_grads.at[core * nch + chip_at(-e), pl.ds(c * crow, crow)]
            as_cp.append(send(ref, ref, as_sem.at[c, e], sib, l))

    for i in range(G_CHUNKS + 4):
        for stage, late in ((loop_reduce, 0), (loop_gather, 1), (chip_gather, 2), (core_gather, 4)):
            if 0 <= i - late < G_CHUNKS:
                stage(i - late)

    for cp in lg_cp:
        cp.wait_recv()
    for k in range(nw):
        out_logits[pl.ds(k, 1), :] = lg_buf[k, :1, :]
    for cp in as_cp:
        cp.wait_recv()
    for cp in sent:
        cp.wait_send()
    for on, make in maybe_sent:
        pl.when(on)(functools.partial(lambda make: make().wait_send(), make))


def body(feats, tiles, tile_rows, tile_cols, tile_count, w_msg, w_self, readout, labels):
    rows_dev, width = feats.shape
    tb = tiles.shape[-1]
    ns = tiles.shape[2]
    nw, nl = lax.axis_size("wide"), lax.axis_size("loop")
    nch = nw // 2
    share = rows_dev // nw
    gshare = width // nch
    cw = width // CHUNKS
    crow = gshare // G_CHUNKS
    prow = crow // nl
    if prow < 16:
        prow = crow
    bf16, f32 = jnp.bfloat16, jnp.float32
    sends = (
        CHUNKS * (nch + 1) + 1 + G_CHUNKS * (nch - 1) + nw - 1 + 2 * G_CHUNKS * (nl - 1)
        + G_CHUNKS * (2 * nch - 1)
    )
    vmem = pl.BlockSpec(memory_space=pltpu.VMEM)
    hbm = pl.BlockSpec(memory_space=pltpu.HBM)
    dma = pltpu.SemaphoreType.DMA
    logits, grads = pl.pallas_call(
        functools.partial(kernel, nl, nw, ns, tb),
        out_shape=(
            pltpu.VMEM((nw, share), f32),
            pltpu.VMEM((nw, gshare, width), bf16),
        ),
        in_specs=[hbm] * 9,
        out_specs=(vmem, vmem),
        scratch_shapes=[
            pltpu.SMEM((ns,), jnp.int32),
            pltpu.SMEM((ns,), jnp.int32),
            pltpu.SMEM((1,), jnp.int32),
            pltpu.VMEM((1, width), f32),
            pltpu.VMEM((nw, share), jnp.int32),
            pltpu.VMEM((CHUNKS, nl * tb, cw), bf16),
            pltpu.VMEM((ns, tb, tb), bf16),
            pltpu.VMEM((2 * share, width), bf16),
            pltpu.VMEM((2 * share, width), bf16),
            pltpu.VMEM((2 * share, width), bf16),
            pltpu.VMEM((width, width), bf16),
            pltpu.VMEM((width, width), bf16),
            pltpu.VMEM((2, nch * share, nl * tb), bf16),
            pltpu.VMEM((CHUNKS, 2, nch * share, cw), bf16),
            pltpu.VMEM((CHUNKS, nch * share, cw), bf16),
            pltpu.VMEM((CHUNKS, nch * share, cw), bf16),
            pltpu.VMEM((CHUNKS, nch - 1, share, cw), bf16),
            pltpu.VMEM((share, width), f32),
            pltpu.VMEM((G_CHUNKS, nch * crow, 2 * share), bf16),
            pltpu.VMEM((G_CHUNKS, nch * crow, width), bf16),
            pltpu.VMEM((G_CHUNKS, nch - 1, crow, width), bf16),
            pltpu.VMEM((G_CHUNKS, crow, width), bf16),
            pltpu.VMEM((G_CHUNKS, nl, prow, width), bf16),
            pltpu.VMEM((nw, 8, share), f32),
            dma((9 + CHUNKS,)),
            dma((sends,)),
            dma((CHUNKS, nl - 1)),
            dma((CHUNKS, nl - 1)),
            dma((CHUNKS, nl - 1)),
            dma((CHUNKS, nl - 1)),
            dma((CHUNKS,)),
            dma((CHUNKS, nch - 1)),
            dma((CHUNKS,)),
            dma((1,)),
            dma((G_CHUNKS, nch - 1)),
            dma((G_CHUNKS, nl - 1)),
            dma((G_CHUNKS, nl - 1)),
            dma((G_CHUNKS, nch - 1)),
            dma((G_CHUNKS, nch)),
            dma((nw - 1,)),
        ],
        compiler_params=pltpu.CompilerParams(
            collective_id=0, has_side_effects=True, vmem_limit_bytes=60 * 2**20
        ),
    )(
        feats, tiles.reshape(ns, tb, tb), tile_rows.reshape(ns), tile_cols.reshape(ns),
        tile_count.reshape(1), w_msg, w_self, readout.reshape(1, width),
        labels.reshape(nw, share),
    )
    both = grads.reshape(2, width, width)
    return logits.reshape(rows_dev), both[0], both[1]


def solution(mesh):
    placed = (
        P("loop", None),
        P("loop", "wide", None, None, None),
        P("loop", "wide", None),
        P("loop", "wide", None),
        P("loop", "wide"),
        P(),
        P(),
        P(),
        P("loop"),
    )
    return jax.shard_map(
        body, mesh=mesh, in_specs=placed, out_specs=(P("loop"), P(), P()), check_vma=False
    )
```

```python
import functools

import jax
import jax.numpy as jnp
from jax import lax
from jax.experimental import pallas as pl
from jax.experimental.pallas import tpu as pltpu
from jax.sharding import PartitionSpec as P

CHUNKS = 2
G_CHUNKS = 2
ROW_STEP = 32


def kernel(
    nl, nw, ns, tb,
    feats, tiles, rows_in, cols_in, count_in, w_msg, w_self, readout_in, labels_in,
    out_logits, out_grads,
    t_rows, t_cols, t_count, readout, labels,
    gath, tiles_v, nf2, msg2, pg2, wm_v, ws_v, adj, part, sib_in, plane_out, plane_in, pre, trans,
    g_out, g_in, z_out, z_in, lg_buf,
    local_sem, send_sem, right_send, left_send, right_sem, left_sem, rs_sib_sem, rs_pl_sem, msg_sem, pg_sem, g_pl_sem, zr_sem, za_sem,
    ap_sem, as_sem, lg_sem,
):
    f32, bf16 = jnp.float32, jnp.bfloat16
    rows_dev, width = feats.shape
    nb = rows_dev // tb
    nch = nw // 2
    share = rows_dev // nw
    gshare = width // nch
    cw = width // CHUNKS
    crow = gshare // G_CHUNKS
    prow = z_in.shape[2]
    pieces = crow // prow
    w = lax.axis_index("wide")
    l = lax.axis_index("loop")
    core = lax.rem(w, 2)
    chip = lax.div(w, 2)
    other = 1 - core
    sib = chip * 2 + other

    def cols(c):
        return pl.ds(c * cw, cw)

    def block_rows(q):
        return pl.ds(pl.multiple_of(q * tb, tb), tb)

    locs = [
        pltpu.make_async_copy(tiles, tiles_v, local_sem.at[0]),
        pltpu.make_async_copy(
            feats.at[pl.ds(pl.multiple_of(chip * 2 * share, 2 * share), 2 * share)], nf2,
            local_sem.at[1],
        ),
        pltpu.make_async_copy(w_self, ws_v, local_sem.at[2]),
        pltpu.make_async_copy(w_msg, wm_v, local_sem.at[3]),
        pltpu.make_async_copy(rows_in, t_rows, local_sem.at[4]),
        pltpu.make_async_copy(cols_in, t_cols, local_sem.at[5]),
        pltpu.make_async_copy(readout_in, readout, local_sem.at[6]),
        pltpu.make_async_copy(labels_in, labels, local_sem.at[7]),
        pltpu.make_async_copy(count_in, t_count, local_sem.at[8]),
    ]
    own_rows = pl.ds(pl.multiple_of(lax.rem(w, nb) * tb, tb), tb)
    own_copies = []
    for c in range(CHUNKS):
        own_copies.append(pltpu.make_async_copy(
            feats.at[own_rows, cols(c)],
            gath.at[c, block_rows(l)],
            local_sem.at[9 + c],
        ))
    for cp in own_copies + locs:
        cp.start()

    barrier = pltpu.get_barrier_semaphore()
    for d in range(1, nw):
        pl.semaphore_signal(barrier, inc=1, device_id={"wide": lax.rem(w + d, nw), "loop": l},
                            device_id_type=pl.DeviceIdType.MESH)
    for d in range(1, nl):
        pl.semaphore_signal(barrier, inc=1, device_id={"wide": w, "loop": lax.rem(l + d, nl)},
                            device_id_type=pl.DeviceIdType.MESH)
    pl.semaphore_wait(barrier, nw + nl - 2)

    sent = []

    def send(src, dst, recv, wide, loop):
        cp = pltpu.make_async_remote_copy(
            src_ref=src, dst_ref=dst, send_sem=send_sem.at[len(sent)], recv_sem=recv,
            device_id={"wide": wide, "loop": loop}, device_id_type=pl.DeviceIdType.MESH,
        )
        cp.start()
        sent.append(cp)
        return cp

    def chip_at(e):
        return lax.rem(chip + e + nch, nch)

    def loop_at(d):
        return lax.rem(l + d + nl, nl)

    maybe_sent = []

    def send_if(on, src, c, block, dist, to_right, step):
        send_s = (right_send if to_right else left_send).at[c, dist - 1]
        recv_s = (right_sem if to_right else left_sem).at[c, dist - 1]

        def make():
            return pltpu.make_async_remote_copy(
                src_ref=src(), dst_ref=gath.at[c, block_rows(block)], send_sem=send_s, recv_sem=recv_s,
                device_id={"wide": w, "loop": l + step if to_right else l - step},
                device_id_type=pl.DeviceIdType.MESH,
            )

        @pl.when(on)
        def _():
            make().start()

        maybe_sent.append((on, make))

    def wait_if(on, c, dist, from_left):
        @pl.when(on)
        def _():
            ref = gath.at[c, block_rows(l - dist if from_left else l + dist)]
            pltpu.make_async_remote_copy(
                src_ref=ref, dst_ref=ref, send_sem=send_sem.at[0],
                recv_sem=(right_sem if from_left else left_sem).at[c, dist - 1],
                device_id={"wide": w, "loop": l - 1 if from_left else l + 1},
                device_id_type=pl.DeviceIdType.MESH,
            ).wait_recv()

    relayed = range(2, nl - 1)

    def direct(c):
        own_copies[c].wait()
        own = functools.partial(lambda c: gath.at[c, block_rows(l)], c)
        for d in (2, 1):
            if d < nl:
                send_if(l + d < nl, own, c, l, d, True, d)
                send_if(l >= d, own, c, l, d, False, d)

    for c in range(CHUNKS - 1):
        direct(c)

    def relay(c):
        for t in relayed:
            wait_if(l >= t, c, t, True)
            send_if(jnp.logical_and(l >= t, l + 1 < nl),
                    functools.partial(lambda c, t: gath.at[c, block_rows(l - t)], c, t),
                    c, l - t, t + 1, True, 1)
            wait_if(l + t < nl, c, t, False)
            send_if(jnp.logical_and(l + t < nl, l >= 1),
                    functools.partial(lambda c, t: gath.at[c, block_rows(l + t)], c, t),
                    c, l + t, t + 1, False, 1)

    def gathered(c):
        for t in range(1, nl):
            if t not in relayed:
                wait_if(l >= t, c, t, True)
                wait_if(l + t < nl, c, t, False)

    for k in (0, 4, 5, 8):
        locs[k].wait()
    cell = [
        jnp.where(s < t_count[0], t_rows[s] * nl + t_cols[s], -1) for s in range(ns)
    ]
    group = 4
    steps = tb // ROW_STEP

    def densify(i, carry):
        r = lax.div(i, steps)
        h = lax.rem(i, steps)
        first = r * tb + h * ROW_STEP
        share_id = lax.div(first, share)
        at = lax.div(share_id, 2) * share + lax.rem(first, share)
        for q0 in range(0, nl, group):
            accs = [jnp.zeros((ROW_STEP, tb), f32) for _ in range(group)]
            for s in range(ns):
                t = tiles_v[s, pl.ds(pl.multiple_of(h * ROW_STEP, ROW_STEP), ROW_STEP), :].astype(f32)
                for g in range(group):
                    on = jnp.where(cell[s] == r * nl + q0 + g, 1.0, 0.0).astype(f32)
                    accs[g] = accs[g] + on * t
            for g in range(group):
                adj[lax.rem(share_id, 2), pl.ds(pl.multiple_of(at, ROW_STEP), ROW_STEP),
                    pl.ds((q0 + g) * tb, tb)] = accs[g].astype(bf16)
        return carry

    lax.fori_loop(0, nb * steps // 2, densify, 0)
    relay(0)
    direct(CHUNKS - 1)
    lax.fori_loop(nb * steps // 2, nb * steps, densify, 0)
    relay(1)

    sib_cp, pl_cp = [], []

    def partial_of(c):
        gathered(c)
        part[c, other] = jnp.dot(adj[other], gath[c], preferred_element_type=f32).astype(bf16)
        sib_cp.append(send(part.at[c, other], sib_in.at[c], rs_sib_sem.at[c], sib, l))
        part[c, core] = jnp.dot(adj[core], gath[c], preferred_element_type=f32).astype(bf16)

    def pair_sum(c, mine, theirs, out):
        out[c] = (mine[c, core].astype(f32) + theirs[c].astype(f32)).astype(bf16)

    def spread(c, out, land, sems, size):
        return [
            send(out.at[c, pl.ds(pl.multiple_of(chip_at(e) * size, size), size)],
                 land.at[c, e - 1], sems.at[c, e - 1], chip_at(e) * 2 + core, l)
            for e in range(1, nch)
        ]

    def total(c, out, land, size):
        acc = out[c, pl.ds(pl.multiple_of(chip * size, size), size), :].astype(f32)
        for e in range(1, nch):
            acc = acc + land[c, e - 1].astype(f32)
        return acc

    def to_chips(c):
        sib_cp[c].wait_recv()
        pair_sum(c, part, sib_in, plane_out)
        pl_cp.append(spread(c, plane_out, plane_in, rs_pl_sem, share))

    partial_of(0)
    for c in range(2, CHUNKS):
        relay(c)
        partial_of(c - 1)
        to_chips(c - 2)
    partial_of(CHUNKS - 1)
    to_chips(CHUNKS - 2)
    to_chips(CHUNKS - 1)

    for k in (1, 2, 3, 6, 7):
        locs[k].wait()
    mine = pl.ds(pl.multiple_of(core * share, share), share)
    nf = nf2[mine, :]
    pre[...] = jnp.dot(nf, ws_v[...], preferred_element_type=f32)

    def put_trans(first, block):
        for j in range(block.shape[0] // crow):
            k, at = divmod(first + j * crow, gshare)
            trans[at // crow, pl.ds(k * crow, crow), :] = block[j * crow:(j + 1) * crow]

    def msg_trans(c):
        msg_cp[c].wait_recv()

        @pl.when(core == 0)
        def _():
            put_trans(c * cw, msg2[:, cols(c)].astype(f32).T.astype(bf16))

    @pl.when(core == 1)
    def _():
        put_trans(0, nf2[...].astype(f32).T.astype(bf16))

    label_col = jnp.broadcast_to(
        labels[pl.ds(w, 1), :].astype(f32), (128, share)).T[:, :1]

    msg_cp = []
    for c in range(CHUNKS):
        for cp in pl_cp[c]:
            cp.wait_recv()
        msg = total(c, plane_out, plane_in, share).astype(bf16)
        pre[...] += jnp.dot(msg, wm_v[pl.ds(c * cw, cw), :], preferred_element_type=f32)
        msg2[mine, cols(c)] = msg
        ref = msg2.at[mine, cols(c)]
        msg_cp.append(send(ref, ref, msg_sem.at[c], sib, l))
        if c > 0:
            msg_trans(c - 1)

    act = pre[...]
    gate = jax.nn.sigmoid(act)
    ro = readout[...]
    hidden = nf.astype(f32) + act * gate
    logit = jnp.sum(hidden * ro, axis=1, keepdims=True)
    resid = jax.nn.sigmoid(logit) - label_col
    pg = (resid * ro * gate * (1.0 + act * (1.0 - gate))).astype(bf16)

    pg2[mine, :] = pg
    ref = pg2.at[mine]
    pg_cp = send(ref, ref, pg_sem.at[0], sib, l)
    msg_trans(CHUNKS - 1)
    pg_cp.wait_recv()

    pl_cp = []
    for c in range(G_CHUNKS):
        g_out[c] = jnp.dot(trans[c], pg2[...], preferred_element_type=f32).astype(bf16)
        pl_cp.append(spread(c, g_out, g_in, g_pl_sem, crow))
    lg_buf[w] = jnp.broadcast_to(logit, (share, 128)).T[:8, :]
    lg_cp = [send(lg_buf.at[w], lg_buf.at[w], lg_sem.at[d - 1], lax.rem(w + d, nw), l)
             for d in range(1, nw)]

    zr_cp, za_cp, ap_cp, as_cp = [], [], [], []

    def loop_reduce(c):
        for cp in pl_cp[c]:
            cp.wait_recv()
        z_out[c] = total(c, g_out, g_in, crow).astype(bf16)
        cps = []
        for d in range(1, nl):
            src = z_out.at[c]
            if pieces > 1:
                src = z_out.at[c, pl.ds(pl.multiple_of(loop_at(d) * prow, prow), prow)]
            cps.append(send(src, z_in.at[c, l], zr_sem.at[c, d - 1], w, loop_at(d)))
        zr_cp.append(cps)
        if pieces > 1:
            z_in[c, l] = z_out[c, pl.ds(pl.multiple_of(l * prow, prow), prow), :]
        else:
            z_in[c, l] = z_out[c]

    def loop_gather(c):
        for cp in zr_cp[c]:
            cp.wait_recv()
        acc = z_in[c, 0].astype(f32)
        for k in range(1, nl):
            acc = acc + z_in[c, k].astype(f32)
        at = l * prow if pieces > 1 else 0
        rws = pl.ds(pl.multiple_of(c * crow + at, prow), prow)
        out_grads[core * nch + chip, rws, :] = acc.astype(bf16)
        ref = out_grads.at[core * nch + chip, rws]
        za_cp.append([send(ref, ref, za_sem.at[c, d - 1], w, loop_at(d))
                      for d in range(1, nl)] if pieces > 1 else [])

    def chip_gather(c):
        for cp in za_cp[c]:
            cp.wait_recv()
        ref = out_grads.at[core * nch + chip, pl.ds(c * crow, crow)]
        ap_cp.append([send(ref, ref, ap_sem.at[c, e - 1], chip_at(e) * 2 + core, l)
                      for e in range(1, nch)])
        as_cp.append(send(ref, ref, as_sem.at[c, 0], sib, l))

    def core_gather(c):
        for e in range(1, nch):
            ap_cp[c][e - 1].wait_recv()
            ref = out_grads.at[core * nch + chip_at(-e), pl.ds(c * crow, crow)]
            as_cp.append(send(ref, ref, as_sem.at[c, e], sib, l))

    for i in range(G_CHUNKS + 4):
        for stage, late in ((loop_reduce, 0), (loop_gather, 1), (chip_gather, 2), (core_gather, 4)):
            if 0 <= i - late < G_CHUNKS:
                stage(i - late)

    for cp in lg_cp:
        cp.wait_recv()
    for k in range(nw):
        out_logits[pl.ds(k, 1), :] = lg_buf[k, :1, :]
    for cp in as_cp:
        cp.wait_recv()
    for cp in sent:
        cp.wait_send()
    for on, make in maybe_sent:
        pl.when(on)(functools.partial(lambda make: make().wait_send(), make))


def body(feats, tiles, tile_rows, tile_cols, tile_count, w_msg, w_self, readout, labels):
    rows_dev, width = feats.shape
    tb = tiles.shape[-1]
    ns = tiles.shape[2]
    nw, nl = lax.axis_size("wide"), lax.axis_size("loop")
    nch = nw // 2
    share = rows_dev // nw
    gshare = width // nch
    cw = width // CHUNKS
    crow = gshare // G_CHUNKS
    prow = crow // nl
    if prow < 16:
        prow = crow
    bf16, f32 = jnp.bfloat16, jnp.float32
    sends = (
        CHUNKS * (nch + 1) + 1 + G_CHUNKS * (nch - 1) + nw - 1 + 2 * G_CHUNKS * (nl - 1)
        + G_CHUNKS * (2 * nch - 1)
    )
    vmem = pl.BlockSpec(memory_space=pltpu.VMEM)
    hbm = pl.BlockSpec(memory_space=pltpu.HBM)
    dma = pltpu.SemaphoreType.DMA
    logits, grads = pl.pallas_call(
        functools.partial(kernel, nl, nw, ns, tb),
        out_shape=(
            pltpu.VMEM((nw, share), f32),
            pltpu.VMEM((nw, gshare, width), bf16),
        ),
        in_specs=[hbm] * 9,
        out_specs=(vmem, vmem),
        scratch_shapes=[
            pltpu.SMEM((ns,), jnp.int32),
            pltpu.SMEM((ns,), jnp.int32),
            pltpu.SMEM((1,), jnp.int32),
            pltpu.VMEM((1, width), f32),
            pltpu.VMEM((nw, share), jnp.int32),
            pltpu.VMEM((CHUNKS, nl * tb, cw), bf16),
            pltpu.VMEM((ns, tb, tb), bf16),
            pltpu.VMEM((2 * share, width), bf16),
            pltpu.VMEM((2 * share, width), bf16),
            pltpu.VMEM((2 * share, width), bf16),
            pltpu.VMEM((width, width), bf16),
            pltpu.VMEM((width, width), bf16),
            pltpu.VMEM((2, nch * share, nl * tb), bf16),
            pltpu.VMEM((CHUNKS, 2, nch * share, cw), bf16),
            pltpu.VMEM((CHUNKS, nch * share, cw), bf16),
            pltpu.VMEM((CHUNKS, nch * share, cw), bf16),
            pltpu.VMEM((CHUNKS, nch - 1, share, cw), bf16),
            pltpu.VMEM((share, width), f32),
            pltpu.VMEM((G_CHUNKS, nch * crow, 2 * share), bf16),
            pltpu.VMEM((G_CHUNKS, nch * crow, width), bf16),
            pltpu.VMEM((G_CHUNKS, nch - 1, crow, width), bf16),
            pltpu.VMEM((G_CHUNKS, crow, width), bf16),
            pltpu.VMEM((G_CHUNKS, nl, prow, width), bf16),
            pltpu.VMEM((nw, 8, share), f32),
            dma((9 + CHUNKS,)),
            dma((sends,)),
            dma((CHUNKS, nl - 1)),
            dma((CHUNKS, nl - 1)),
            dma((CHUNKS, nl - 1)),
            dma((CHUNKS, nl - 1)),
            dma((CHUNKS,)),
            dma((CHUNKS, nch - 1)),
            dma((CHUNKS,)),
            dma((1,)),
            dma((G_CHUNKS, nch - 1)),
            dma((G_CHUNKS, nl - 1)),
            dma((G_CHUNKS, nl - 1)),
            dma((G_CHUNKS, nch - 1)),
            dma((G_CHUNKS, nch)),
            dma((nw - 1,)),
        ],
        compiler_params=pltpu.CompilerParams(
            collective_id=0, has_side_effects=True, vmem_limit_bytes=60 * 2**20
        ),
    )(
        feats, tiles.reshape(ns, tb, tb), tile_rows.reshape(ns), tile_cols.reshape(ns),
        tile_count.reshape(1), w_msg, w_self, readout.reshape(1, width),
        labels.reshape(nw, share),
    )
    both = grads.reshape(2, width, width)
    return logits.reshape(rows_dev), both[0], both[1]


def solution(mesh):
    placed = (
        P("loop", None),
        P("loop", "wide", None, None, None),
        P("loop", "wide", None),
        P("loop", "wide", None),
        P("loop", "wide"),
        P(),
        P(),
        P(),
        P("loop"),
    )
    return jax.shard_map(
        body, mesh=mesh, in_specs=placed, out_specs=(P("loop"), P(), P()), check_vma=False
    )
```
